512 devices in a mesh: row: 32 (over y, x, core), col: 16 (over z).
Axes of the slice: x: 4, y: 4, z: 16, core: 2. Of those that a mesh axis runs over, the one named last changes fastest.
Arguments:
- inverse_cov: float32 [18432, 18432], P('row', 'col'), as said below
- key_table: bfloat16 [1024, 18432], P(None, 'row'), may hold values from -6 to 6
- weight: bfloat16 [18432, 7168], P('row', 'col'), may hold values from -0.046875 to 0.046875
- edit_index: int32 [2, 256], replicated, may hold values from 0 to 1023
- targets: bfloat16 [2, 256, 7168], P(None, None, 'col'), may hold values from -24 to 24
Outputs:
- weight_change: bfloat16 [18432, 7168], P('row', 'col')
The draws below stay inside these ranges and needn't reach their ends.
Inputs may be any that keep to these rules, and one draw needn't show every extreme that they name: inverse_cov is symmetric and positive definite.
All inputs are finite; a program needn't handle non-finite values.
Results may differ from the reference program's by a relative error of at most 0.001.
Values may be sent and summed in bfloat16 or wider, within the bound.
No kernel may reach another device: no remote copies, remote signals or barrier semaphores. Data moves between devices by JAX's collectives and lax.ppermute only.
A program may use at most 64 MiB of HBM per device.

```python
import math
import jax
import jax.numpy as jnp
from jax import lax

F = 18432
D = 7168
KEYS = 256
TABLE_ROWS = 1024


def draw_inverse_cov(key, part):
    key_main = jax.random.fold_in(key, 11)
    spread = 0.375 * math.sqrt(6.0 / F)
    raw_noise = jax.random.uniform(key_main, (F, F), jnp.float32, -spread, spread)
    matrix = jnp.eye(F, dtype=jnp.float32) + 0.5 * (raw_noise + raw_noise.T)
    return matrix / F


def touch_ends(drawn, stream_key, smallest, top_value):
    spot = [jax.random.randint(jax.random.fold_in(stream_key, axis), (), 0, length) for axis, length in enumerate(drawn.shape)]
    longest = drawn.shape.index(max(drawn.shape))
    next_to = spot[:longest] + [(spot[longest] + 1) % drawn.shape[longest]] + spot[longest + 1:]
    return drawn.at[tuple(spot)].set(smallest).at[tuple(next_to)].set(top_value)


def block_levels(stream_key, shape, pieces, least, largest):
    factor_of = 1.0
    for axis_at, shards_of in pieces:
        draws = jax.random.uniform(jax.random.fold_in(jax.random.fold_in(stream_key, 6), axis_at), (shards_of,), jnp.float32, least / len(pieces), largest / len(pieces))
        factor_of = factor_of * jnp.repeat(jnp.exp(draws), shape[axis_at] // shards_of).reshape((-1,) + (1,) * (len(shape) - 1 - axis_at))
    return factor_of


def normal_values(key, shape, scale, reach, pieces=(), held_as=jnp.bfloat16):
    entries = scale * jax.random.normal(key, shape, jnp.float32)
    if pieces:
        entries = entries * block_levels(key, shape, pieces, -0.22, 0.18)
    return jnp.clip(entries, -reach, reach).astype(held_as)


def setup_inputs(seed: int = 0) -> dict:
    seeds = jax.random.split(jax.random.key(seed), 6)
    return {
        "inverse_cov": draw_inverse_cov(jax.random.fold_in(seeds[5], 71), 0),
        "key_table": normal_values(seeds[1], (TABLE_ROWS, F), 1.0, 6.0, ((1, 32),)),
        "weight": normal_values(seeds[2], (F, D), F ** -0.5, 0.046875, ((0, 32), (1, 16))),
        "edit_index": touch_ends(jax.random.randint(seeds[3], (2, KEYS), 0, TABLE_ROWS), jax.random.fold_in(seeds[3], 1), 0, TABLE_ROWS - 1).astype(jnp.int32),
        "targets": normal_values(seeds[4], (2, KEYS, D), 4.0, 24.0, ((2, 16),)),
    }


def reference(inverse_cov, key_table, weight, edit_index, targets):
    highest = lax.Precision.HIGHEST
    first_keys = jnp.take(key_table, edit_index[0].astype(jnp.int32), axis=0)
    second_keys = jnp.take(key_table, edit_index[1].astype(jnp.int32), axis=0)
    first_f = first_keys.astype(jnp.float32)
    second_f = second_keys.astype(jnp.float32)
    identity = jnp.eye(KEYS, dtype=jnp.float32)
    first_panel = jnp.dot(inverse_cov, first_f.T, precision=highest)
    system_one = identity + jnp.dot(first_f, first_panel, precision=highest)
    factor_one = jnp.linalg.cholesky(system_one)
    residual_one = targets[0].astype(jnp.float32) - jnp.dot(first_keys.astype(jnp.float32), weight.astype(jnp.float32), preferred_element_type=jnp.float32)
    solved_one = jax.scipy.linalg.cho_solve((factor_one, True), residual_one)
    delta_one = jnp.dot(first_panel, solved_one, precision=highest)
    raw_second = jnp.dot(inverse_cov, second_f.T, precision=highest)
    cross_terms = jnp.dot(first_panel.T, second_f.T, precision=highest)
    second_panel = raw_second - jnp.dot(first_panel, jax.scipy.linalg.cho_solve((factor_one, True), cross_terms), precision=highest)
    system_two = identity + jnp.dot(second_f, second_panel, precision=highest)
    factor_two = jnp.linalg.cholesky(system_two)
    second_out = jnp.dot(second_keys.astype(jnp.float32), weight.astype(jnp.float32), preferred_element_type=jnp.float32) + jnp.dot(second_f, delta_one, precision=highest)
    residual_two = targets[1].astype(jnp.float32) - second_out
    solved_two = jax.scipy.linalg.cho_solve((factor_two, True), residual_two)
    delta_two = jnp.dot(second_panel, solved_two, precision=highest)
    return (math.sqrt(F) * (delta_one + delta_two)).astype(jnp.bfloat16)
```

```python
import math

import jax
import jax.numpy as jnp
from jax import lax
from jax.experimental import pallas as pl
from jax.experimental.pallas import tpu as pltpu
from jax.sharding import PartitionSpec as P

F = 18432
LANES = 128
HIGHEST = lax.Precision.HIGHEST


def split(value):
    high = value.astype(jnp.bfloat16)
    return high, (value - high.astype(jnp.float32)).astype(jnp.bfloat16)


def dot16(a, b):
    return jnp.dot(a, b, preferred_element_type=jnp.float32)


def solve_kernel(gram_ref, target_ref, value_ref, out_ref, a_ref, high_ref, low_ref, z_ref, s_ref, r_ref):
    n = a_ref.shape[0]
    blocks = n // LANES
    rows = lax.broadcasted_iota(jnp.int32, (LANES, LANES), 0)
    cols = lax.broadcasted_iota(jnp.int32, (LANES, LANES), 1)
    eye = jnp.where(rows == cols, 1.0, 0.0).astype(jnp.float32)
    place = 0
    for i in range(blocks):
        for j in range(i + 1):
            block = gram_ref[place * LANES:(place + 1) * LANES, :]
            place += 1
            if i == j:
                a_ref[i * LANES:(i + 1) * LANES, j * LANES:(j + 1) * LANES] = block + eye
            else:
                a_ref[i * LANES:(i + 1) * LANES, j * LANES:(j + 1) * LANES] = block
                a_ref[j * LANES:(j + 1) * LANES, i * LANES:(i + 1) * LANES] = block.T
    a = a_ref[...]
    top = jnp.maximum(jnp.max(jnp.sum(jnp.abs(a), axis=0)), 1.0)
    r_ref[...] = target_ref[...].astype(jnp.float32) - value_ref[...]
    big_rows = lax.broadcasted_iota(jnp.int32, (n, n), 0)
    big_cols = lax.broadcasted_iota(jnp.int32, (n, n), 1)
    one = jnp.where(big_rows == big_cols, 1.0, 0.0).astype(jnp.float32)
    middle = top + 1.0
    width = top - 1.0
    scale = 2.0 * middle * middle - width * width
    first, second = 8.0 * middle / scale, 8.0 / scale
    rho = width * width / scale
    limit = jnp.max(jnp.abs(r_ref[...])) * 1e-5

    def refine(residual_of, apply):
        def more(carry):
            step, worst = carry
            return jnp.logical_and(step < 12, worst > limit)

        def body(carry):
            step, _ = carry
            residual = residual_of(out_ref[...])
            out_ref[...] += apply(residual)
            return step + 1, jnp.max(jnp.abs(residual))

        lax.while_loop(more, body, (jnp.int32(0), 2.0 * limit))

    @pl.when(top <= 32.0)
    def _():
        high, low = split(a)
        high_ref[...] = high
        low_ref[...] = low
        s_ref[...] = one - first * a + second * dot16(high, high)
        z_ref[...] = first * one - second * a

        def body(rho):
            s16 = s_ref[...].astype(jnp.bfloat16)
            z16 = z_ref[...].astype(jnp.bfloat16)
            z_ref[...] += dot16(z16, s16)
            s_ref[...] = dot16(s16, s16)
            return rho * rho

        lax.while_loop(lambda rho: rho > 0.004, body, rho)
        high_ref2 = z_ref[...].astype(jnp.bfloat16)
        s_ref[...] = high_ref2.astype(jnp.float32)
        out_ref[...] = dot16(high_ref2, r_ref[...].astype(jnp.bfloat16))

        def residual_of(y):
            y_high, y_low = split(y)
            return r_ref[...] - (
                dot16(high_ref[...], y_high) + (dot16(high_ref[...], y_low) + dot16(low_ref[...], y_high))
            )

        refine(residual_of, lambda res: dot16(s_ref[...].astype(jnp.bfloat16), res.astype(jnp.bfloat16)))

    @pl.when(top > 32.0)
    def _():
        def full(x, y):
            return jnp.dot(x, y, precision=HIGHEST, preferred_element_type=jnp.float32)

        z_ref[...] = first * one - second * a

        def body(carry):
            rho, extra = carry
            s_ref[...] = one - full(a_ref[...], z_ref[...])
            z_ref[...] += full(z_ref[...], s_ref[...])
            return rho * rho, jnp.where(rho < 0.01, extra + 1, extra)

        lax.while_loop(lambda carry: carry[1] < 2, body, (rho, jnp.int32(0)))
        out_ref[...] = full(z_ref[...], r_ref[...])
        refine(lambda y: r_ref[...] - full(a_ref[...], y), lambda res: full(z_ref[...], res))


def solve(gram_packed, targets, values):
    n, width = targets.shape
    square = pltpu.VMEM((n, n), jnp.float32)
    half = pltpu.VMEM((n, n), jnp.bfloat16)
    return pl.pallas_call(
        solve_kernel,
        out_shape=jax.ShapeDtypeStruct((n, width), jnp.float32),
        in_specs=[pl.BlockSpec(memory_space=pltpu.VMEM)] * 3,
        out_specs=pl.BlockSpec(memory_space=pltpu.VMEM),
        scratch_shapes=[square, half, half, square, square, pltpu.VMEM((n, width), jnp.float32)],
        compiler_params=pltpu.CompilerParams(vmem_limit_bytes=48 * 2**20),
    )(gram_packed, targets, values)


def dot_exact_right(a, b16, dims):
    high = lax.reduce_precision(a, 8, 7)
    low = a - high
    out = lax.dot_general(high.astype(jnp.bfloat16), b16, dims, preferred_element_type=jnp.float32)
    return out + lax.dot_general(low.astype(jnp.bfloat16), b16, dims, preferred_element_type=jnp.float32)


def shards(inverse_cov, key_table, weight, edit_index, targets):
    rows = lax.axis_size("row")
    cols = lax.axis_size("col")
    chips = rows // 2
    here, depth = inverse_cov.shape[0], inverse_cov.shape[1]
    n = edit_index.size
    width = weight.shape[1]
    piece = here // chips
    core = lax.axis_index("row") % 2
    table_rows = key_table.shape[0]
    turned = [((2 * a + h) * cols + b, (2 * b + h) * cols + a) for a in range(chips) for b in range(cols) for h in range(2)]
    same_core = [[2 * k + h for k in range(chips)] for h in range(2)]
    other_core = [(r, r ^ 1) for r in range(rows)]

    picked = (lax.broadcasted_iota(jnp.int32, (table_rows, n), 0) == edit_index.reshape(1, n)).astype(jnp.bfloat16)
    keys = lax.dot_general(key_table, picked, (((0,), (0,)), ((), ()))).astype(jnp.bfloat16)
    key_slice = lax.dynamic_slice_in_dim(keys, lax.axis_index("col") * piece, piece, 0)
    key_piece = lax.ppermute(key_slice, ("row", "col"), turned)

    part = dot_exact_right(inverse_cov, keys, (((0,), (0,)), ((), ())))
    value = lax.dot_general(keys, weight, (((0,), (0,)), ((), ())), preferred_element_type=jnp.float32)
    part = part.reshape(2, chips, piece, n)
    value = jnp.pad(value, ((0, 0), (0, n - width))).reshape(chips, 2, n // rows, n)

    def half(which):
        return jnp.concatenate(
            [
                lax.dynamic_index_in_dim(part, which, 0, keepdims=False),
                lax.dynamic_index_in_dim(value, which, 1, keepdims=False),
            ],
            axis=1,
        )

    half_sum = half(core) + lax.ppermute(half(1 - core), "row", other_core)
    received = lax.all_to_all(half_sum, "row", 0, 0, axis_index_groups=same_core, tiled=True)
    summed = jnp.sum(received, axis=0)
    panel_piece = summed[:piece]
    value_piece = summed[piece:, :width]
    values = lax.all_gather(value_piece, "row", axis=0, tiled=True)
    panel_turned = lax.ppermute(panel_piece, ("row", "col"), turned)
    panel = lax.all_gather(panel_turned, "col", axis=0, tiled=True)

    gram_part = lax.dot_general(
        key_piece.astype(jnp.float32), panel_piece, (((0,), (0,)), ((), ())), precision=HIGHEST
    )
    blocks = n // LANES
    packed = jnp.concatenate(
        [
            gram_part[i * LANES:(i + 1) * LANES, j * LANES:(j + 1) * LANES]
            for i in range(blocks)
            for j in range(i + 1)
        ],
        axis=0,
    )
    share = packed.shape[0] // rows
    gram_share = jnp.sum(lax.all_to_all(packed.reshape(rows, share, LANES), "row", 0, 0, tiled=True), axis=0)
    gram_share = jnp.sum(
        lax.all_to_all(jnp.broadcast_to(gram_share, (cols, share, LANES)), "col", 0, 0, tiled=True), axis=0
    )
    gram = lax.all_to_all(jnp.broadcast_to(gram_share, (rows, share, LANES)), "row", 0, 0, tiled=True)
    gram = gram.reshape(rows * share, LANES)
    solved = solve(gram, targets.reshape(n, width), values)
    return (math.sqrt(F) * jnp.dot(panel, solved, precision=HIGHEST)).astype(jnp.bfloat16)


def solution(mesh):
    in_specs = (P("row", "col"), P(None, "row"), P("row", "col"), P(), P(None, None, "col"))
    out_specs = P("row", "col")
    return jax.shard_map(shards, mesh=mesh, in_specs=in_specs, out_specs=out_specs, check_vma=False)
```

```python
import math

import jax
import jax.numpy as jnp
from jax import lax
from jax.experimental import pallas as pl
from jax.experimental.pallas import tpu as pltpu
from jax.sharding import PartitionSpec as P

F = 18432
LANES = 128
VMEM_LIMIT = 48 * 2**20
TALL, SHORT, PADDED = 40, 32, 48
STRIDE = 4
SHIFTS = (0, 1, 2, -1)
HIGHEST = lax.Precision.HIGHEST


def split(value):
    high = value.astype(jnp.bfloat16)
    return high, (value - high.astype(jnp.float32)).astype(jnp.bfloat16)


def dot16(a, b):
    return jnp.dot(a, b, preferred_element_type=jnp.float32)


def solve_kernel(gram_ref, target_ref, value_ref, out_ref, a_ref, high_ref, low_ref, z_ref, s_ref, r_ref):
    n = a_ref.shape[0]
    blocks = n // LANES
    rows = lax.broadcasted_iota(jnp.int32, (LANES, LANES), 0)
    cols = lax.broadcasted_iota(jnp.int32, (LANES, LANES), 1)
    eye = jnp.where(rows == cols, 1.0, 0.0).astype(jnp.float32)
    place = 0
    for i in range(blocks):
        for j in range(i + 1):
            block = gram_ref[place * LANES:(place + 1) * LANES, :]
            place += 1
            if i == j:
                a_ref[i * LANES:(i + 1) * LANES, j * LANES:(j + 1) * LANES] = block + eye
            else:
                a_ref[i * LANES:(i + 1) * LANES, j * LANES:(j + 1) * LANES] = block
                a_ref[j * LANES:(j + 1) * LANES, i * LANES:(i + 1) * LANES] = block.T
    a = a_ref[...]
    top = jnp.maximum(jnp.max(jnp.sum(jnp.abs(a), axis=0)), 1.0)
    r_ref[...] = target_ref[...].astype(jnp.float32) - value_ref[:, :r_ref.shape[1]]
    big_rows = lax.broadcasted_iota(jnp.int32, (n, n), 0)
    big_cols = lax.broadcasted_iota(jnp.int32, (n, n), 1)
    one = jnp.where(big_rows == big_cols, 1.0, 0.0).astype(jnp.float32)
    middle = top + 1.0
    width = top - 1.0
    scale = 2.0 * middle * middle - width * width
    first, second = 8.0 * middle / scale, 8.0 / scale
    rho = width * width / scale
    limit = jnp.max(jnp.abs(r_ref[...])) * 1e-5

    def refine(residual_of, apply):
        def more(carry):
            step, worst = carry
            return jnp.logical_and(step < 12, worst > limit)

        def body(carry):
            step, _ = carry
            residual = residual_of(out_ref[...])
            out_ref[...] += apply(residual)
            return step + 1, jnp.max(jnp.abs(residual))

        lax.while_loop(more, body, (jnp.int32(0), 2.0 * limit))

    @pl.when(top <= 32.0)
    def _():
        high, low = split(a)
        high_ref[...] = high
        low_ref[...] = low
        s_ref[...] = one - first * a + second * dot16(high, high)
        z_ref[...] = first * one - second * a

        def body(rho):
            s16 = s_ref[...].astype(jnp.bfloat16)
            z16 = z_ref[...].astype(jnp.bfloat16)
            z_ref[...] += dot16(z16, s16)
            s_ref[...] = dot16(s16, s16)
            return rho * rho

        lax.while_loop(lambda rho: rho > 0.004, body, rho)
        high_ref2 = z_ref[...].astype(jnp.bfloat16)
        s_ref[...] = high_ref2.astype(jnp.float32)
        out_ref[...] = dot16(high_ref2, r_ref[...].astype(jnp.bfloat16))

        def residual_of(y):
            y_high, y_low = split(y)
            return r_ref[...] - (
                dot16(high_ref[...], y_high) + (dot16(high_ref[...], y_low) + dot16(low_ref[...], y_high))
            )

        refine(residual_of, lambda res: dot16(s_ref[...].astype(jnp.bfloat16), res.astype(jnp.bfloat16)))

    @pl.when(top > 32.0)
    def _():
        def full(x, y):
            return jnp.dot(x, y, precision=HIGHEST, preferred_element_type=jnp.float32)

        z_ref[...] = first * one - second * a

        def body(carry):
            rho, extra = carry
            s_ref[...] = one - full(a_ref[...], z_ref[...])
            z_ref[...] += full(z_ref[...], s_ref[...])
            return rho * rho, jnp.where(rho < 0.01, extra + 1, extra)

        lax.while_loop(lambda carry: carry[1] < 2, body, (rho, jnp.int32(0)))
        out_ref[...] = full(z_ref[...], r_ref[...])
        refine(lambda y: r_ref[...] - full(a_ref[...], y), lambda res: full(z_ref[...], res))


def solve(gram_packed, targets, values):
    n, width = targets.shape
    square = pltpu.VMEM((n, n), jnp.float32)
    half = pltpu.VMEM((n, n), jnp.bfloat16)
    return pl.pallas_call(
        solve_kernel,
        out_shape=jax.ShapeDtypeStruct((n, width), jnp.float32),
        in_specs=[pl.BlockSpec(memory_space=pltpu.VMEM)] * 3,
        out_specs=pl.BlockSpec(memory_space=pltpu.VMEM),
        scratch_shapes=[square, half, half, square, square, pltpu.VMEM((n, width), jnp.float32)],
        compiler_params=pltpu.CompilerParams(vmem_limit_bytes=VMEM_LIMIT),
        cost_estimate=pl.CostEstimate(flops=40 * n * n * n, bytes_accessed=4 * 2**20, transcendentals=0),
    )(gram_packed, targets, values)


def contract_first(a, b):
    return lax.dot_general(a, b, (((0,), (0,)), ((), ())), preferred_element_type=jnp.float32)


def piece_start(index, here, chips):
    return index // 2 * (2 * here // chips) + index % 2 * TALL


def front_kernel(place_ref, index_ref, table_ref, cov_ref, weight_ref, mine_ref, other_ref, slice_ref, part_ref, value_ref):
    here, n = table_ref.shape[1], index_ref.shape[1]
    chips = mine_ref.shape[0]
    width = weight_ref.shape[1]
    core, col = place_ref[0], place_ref[1]
    picked = lax.broadcasted_iota(jnp.int32, (table_ref.shape[0], n), 0) == index_ref[...]
    picked = jnp.where(picked, 1.0, 0.0).astype(jnp.bfloat16)
    keys = contract_first(table_ref[...], picked).astype(jnp.bfloat16)
    padded = slice_ref.shape[0]
    slot = lax.broadcasted_iota(jnp.int32, (padded, here), 0)
    spot = lax.broadcasted_iota(jnp.int32, (padded, here), 1)
    used = TALL - lax.rem(col, 2) * (TALL - SHORT)
    first = lax.div(col, 2) * (TALL + SHORT) + lax.rem(col, 2) * TALL
    taken = jnp.logical_and(slot + first == spot, slot < used)
    taken = jnp.where(taken, 1.0, 0.0).astype(jnp.bfloat16)
    slice_ref[...] = dot16(taken, keys).astype(jnp.bfloat16)
    high, low = split(cov_ref[...])
    part_ref[...] = contract_first(high, keys) + contract_first(low, keys)
    value_ref[...] = contract_first(keys, weight_ref[...])
    for which, ref in ((core, mine_ref), (1 - core, other_ref)):
        for j in range(chips):
            begin = pl.multiple_of(which * here + piece_start(j, here, chips), 8)
            tall = TALL if j % 2 == 0 else SHORT
            ref[j, :tall, :] = part_ref[pl.ds(begin, tall), :]
            if tall < TALL:
                ref[j, tall:TALL, :] = jnp.zeros((TALL - tall, n), jnp.float32)
            share = ref.shape[1] - TALL
            at = pl.multiple_of((2 * j + which) * share, 8)
            ref[j, TALL:, :width] = value_ref[pl.ds(at, share), :]
            ref[j, TALL:, width:] = jnp.zeros((share, n - width), jnp.float32)


def front(place, index, table, cov, weight, chips):
    here, n = table.shape[1], index.shape[1]
    share = n // (2 * chips)
    payload = jax.ShapeDtypeStruct((chips, TALL + share, n), jnp.float32)
    vmem = pl.BlockSpec(memory_space=pltpu.VMEM)
    return pl.pallas_call(
        front_kernel,
        out_shape=(payload, payload, jax.ShapeDtypeStruct((PADDED, n), jnp.bfloat16)),
        in_specs=[pl.BlockSpec(memory_space=pltpu.SMEM)] + [vmem] * 4,
        out_specs=(vmem, vmem, vmem),
        scratch_shapes=[
            pltpu.VMEM((cov.shape[1], n), jnp.float32),
            pltpu.VMEM((n, weight.shape[1]), jnp.float32),
        ],
        compiler_params=pltpu.CompilerParams(vmem_limit_bytes=VMEM_LIMIT),
    )(place, index, table, cov, weight)


def gram_kernel(received_ref, key_ref, panel_ref, value_ref, packed_ref):
    total = received_ref[0]
    for j in range(1, received_ref.shape[0]):
        total = total + received_ref[j]
    panel = total[:TALL]
    panel_ref[...] = panel
    value_ref[...] = total[TALL:]
    n = panel.shape[1]
    padded = jnp.concatenate([panel, jnp.zeros((PADDED - TALL, n), jnp.float32)], axis=0)
    high = padded.astype(jnp.bfloat16)
    rest = padded - high.astype(jnp.float32)
    middle, low = split(rest)
    keys = key_ref[...]
    gram = contract_first(keys, high) + (contract_first(keys, middle) + contract_first(keys, low))
    place = 0
    for i in range(n // LANES):
        for j in range(i + 1):
            packed_ref[place * LANES:(place + 1) * LANES, :] = gram[
                i * LANES:(i + 1) * LANES, j * LANES:(j + 1) * LANES
            ]
            place += 1


def gram_share(received, key_piece):
    n = received.shape[2]
    blocks = n // LANES
    vmem = pl.BlockSpec(memory_space=pltpu.VMEM)
    return pl.pallas_call(
        gram_kernel,
        out_shape=(
            jax.ShapeDtypeStruct((TALL, n), jnp.float32),
            jax.ShapeDtypeStruct((received.shape[1] - TALL, n), jnp.float32),
            jax.ShapeDtypeStruct((blocks * (blocks + 1) // 2 * LANES, LANES), jnp.float32),
        ),
        in_specs=[vmem] * 2,
        out_specs=(vmem, vmem, vmem),
        compiler_params=pltpu.CompilerParams(vmem_limit_bytes=VMEM_LIMIT),
    )(received, key_piece)


def change_kernel(place_ref, *refs):
    *bundle_refs, solved_ref, out_ref, panel_ref = refs
    cols = len(bundle_refs) * STRIDE
    for shift, ref in zip(SHIFTS, bundle_refs):
        for t in range(cols // STRIDE):
            piece = lax.rem(place_ref[1] - shift - STRIDE * t + 2 * cols, cols)
            odd = lax.rem(piece, 2)
            begin = pl.multiple_of(lax.div(piece, 2) * (TALL + SHORT) + odd * TALL, 8)
            panel_ref[pl.ds(begin, SHORT), :] = ref[t * TALL:t * TALL + SHORT, :]

            @pl.when(odd == 0)
            def _(ref=ref, t=t, begin=begin):
                panel_ref[pl.ds(begin + SHORT, TALL - SHORT), :] = ref[t * TALL + SHORT:(t + 1) * TALL, :]

    high, low = split(panel_ref[...])
    solved_high, solved_low = split(solved_ref[...] * math.sqrt(F))
    out = dot16(high, solved_high) + (dot16(high, solved_low) + dot16(low, solved_high))
    out_ref[...] = out.astype(jnp.bfloat16)


def change(place, bundles, solved, here):
    n, width = solved.shape
    vmem = pl.BlockSpec(memory_space=pltpu.VMEM)
    return pl.pallas_call(
        change_kernel,
        out_shape=jax.ShapeDtypeStruct((here, width), jnp.bfloat16),
        in_specs=[pl.BlockSpec(memory_space=pltpu.SMEM)] + [vmem] * (len(bundles) + 1),
        out_specs=vmem,
        scratch_shapes=[pltpu.VMEM((here, n), jnp.float32)],
        compiler_params=pltpu.CompilerParams(vmem_limit_bytes=VMEM_LIMIT),
    )(place, *bundles, solved)


def moved(value, axis, shift):
    size = lax.axis_size(axis)
    return lax.ppermute(value, axis, [(i, (i + shift) % size) for i in range(size)])


def shards(inverse_cov, key_table, weight, edit_index, targets):
    rows = lax.axis_size("row")
    cols = lax.axis_size("col")
    chips = rows // 2
    here = inverse_cov.shape[0]
    n = edit_index.size
    width = weight.shape[1]
    place = jnp.stack([lax.axis_index("row") % 2, lax.axis_index("col")]).astype(jnp.int32)
    turned = [((2 * a + h) * cols + b, (2 * b + h) * cols + a) for a in range(chips) for b in range(cols) for h in range(2)]
    same_core = [[2 * k + h for k in range(chips)] for h in range(2)]
    other_core = [(r, r ^ 1) for r in range(rows)]

    mine, other, key_slice = front(place, edit_index.reshape(1, n), key_table, inverse_cov, weight, chips)
    key_piece = lax.ppermute(key_slice, ("row", "col"), turned)
    half_sum = mine + lax.ppermute(other, "row", other_core)
    received = lax.all_to_all(half_sum, "row", 0, 0, axis_index_groups=same_core, tiled=True)
    panel_piece, value_piece, packed = gram_share(received, key_piece)
    values = lax.all_gather(value_piece, "row", axis=0, tiled=True)

    near = lax.ppermute(panel_piece, ("row", "col"), turned)
    share = packed.shape[0] // rows
    part = jnp.sum(lax.all_to_all(packed.reshape(rows, share, LANES), "row", 0, 0, tiled=True), axis=0)
    part, near = lax.optimization_barrier((part, near))
    far = [moved(near, "col", STRIDE * t) for t in range(1, cols // STRIDE)]
    part = jnp.sum(lax.all_to_all(jnp.broadcast_to(part, (cols, share, LANES)), "col", 0, 0, tiled=True), axis=0)
    part, *far = lax.optimization_barrier((part, *far))
    far = jnp.concatenate([near] + far, axis=0)
    bundles = [far] + [moved(far, "col", shift) for shift in SHIFTS[1:]]
    gram = lax.all_to_all(jnp.broadcast_to(part, (rows, share, LANES)), "row", 0, 0, tiled=True)
    solved = solve(gram.reshape(rows * share, LANES), targets.reshape(n, width), values)
    return change(place, bundles, solved, here)


def solution(mesh):
    in_specs = (P("row", "col"), P(None, "row"), P("row", "col"), P(), P(None, None, "col"))
    out_specs = P("row", "col")
    return jax.shard_map(shards, mesh=mesh, in_specs=in_specs, out_specs=out_specs, check_vma=False)
```

```python
import math

import jax
import jax.numpy as jnp
from jax import lax
from jax.experimental import pallas as pl
from jax.experimental.pallas import tpu as pltpu
from jax.sharding import PartitionSpec as P

F = 18432
LANES = 128
HIGHEST = lax.Precision.HIGHEST
VMEM_LIMIT = 48 * 2**20
TALL, SHORT, PADDED = 40, 32, 48
V_SHORT = 24
STRIDE = 4
SHIFTS = (0, 1, 2, -1)


def split(value):
    high = value.astype(jnp.bfloat16)
    return high, (value - high.astype(jnp.float32)).astype(jnp.bfloat16)


def dot16(a, b):
    return jnp.dot(a, b, preferred_element_type=jnp.float32)


def solve_kernel(gram_ref, target_hbm, value_hbm, high_out, low_out, a_ref, a16_ref, z_ref, s_ref, r_ref, y_ref, target_ref, value_ref, sems):
    n = a_ref.shape[0]
    width = r_ref.shape[0]
    target_copy = pltpu.make_async_copy(target_hbm, target_ref, sems.at[0])
    value_copy = pltpu.make_async_copy(value_hbm, value_ref, sems.at[1])
    target_copy.start()
    value_copy.start()
    blocks = n // LANES
    rows = lax.broadcasted_iota(jnp.int32, (LANES, LANES), 0)
    cols = lax.broadcasted_iota(jnp.int32, (LANES, LANES), 1)
    eye = jnp.where(rows == cols, 1.0, 0.0).astype(jnp.float32)
    place = 0
    for i in range(blocks):
        for j in range(i + 1):
            block = gram_ref[place * LANES:(place + 1) * LANES, :]
            place += 1
            if i == j:
                a_ref[i * LANES:(i + 1) * LANES, j * LANES:(j + 1) * LANES] = block + eye
            else:
                a_ref[i * LANES:(i + 1) * LANES, j * LANES:(j + 1) * LANES] = block
                a_ref[j * LANES:(j + 1) * LANES, i * LANES:(i + 1) * LANES] = block.T
    a = a_ref[...]
    top = jnp.maximum(jnp.max(jnp.sum(jnp.abs(a), axis=0)), 1.0)
    high = a.astype(jnp.bfloat16)
    a16_ref[0] = high
    a16_ref[1] = (a - high.astype(jnp.float32)).astype(jnp.bfloat16)
    middle = top + 1.0
    span = top - 1.0
    scale = 2.0 * middle * middle - span * span
    first, second = 8.0 * middle / scale, 8.0 / scale
    rho = span * span / scale

    def add_eye(ref, times):
        for i in range(blocks):
            at = slice(i * LANES, (i + 1) * LANES)
            ref[at, at] += eye * times

    def load_residual():
        target_copy.wait()
        value_copy.wait()
        per_batch = target_ref.shape[2]
        share = value_ref.shape[1]
        for b in range(target_ref.shape[0]):
            r_ref[:, b * per_batch:(b + 1) * per_batch] = target_ref[b].astype(jnp.float32)
        half = n // 2
        for r in range(value_ref.shape[0]):
            k, h = r // 2, r % 2
            tall = 2 * share if k % 2 == 0 else V_SHORT
            begin = k // 2 * (2 * share + V_SHORT) + k % 2 * 2 * share
            at = slice(h * half, (h + 1) * half)
            r_ref[begin:begin + share, at] -= value_ref[r, :, :half]
            r_ref[begin + share:begin + tall, at] -= value_ref[r, :tall - share, half:]

    def more(carry):
        step, before, worst, limit = carry
        return jnp.logical_and(step < 12, worst * worst > limit * before)

    def finish():
        result = y_ref[...] * math.sqrt(F)
        high, low = split(result)
        high_out[...] = high
        low_out[...] = low

    @pl.when(top <= 32.0)
    def _():
        z_ref[...] = -second * a_ref[...]
        add_eye(z_ref, first)
        s_ref[...] = second * dot16(a16_ref[0], a16_ref[0]) - first * a_ref[...]
        add_eye(s_ref, 1.0)

        def body(rho):
            s16 = s_ref[...].astype(jnp.bfloat16)
            both = dot16(jnp.concatenate([z_ref[...].astype(jnp.bfloat16), s16], axis=0), s16)
            z_ref[...] += both[:n]
            s_ref[...] = both[n:]
            return rho * rho

        lax.while_loop(lambda rho: rho * rho > 0.004, body, rho)
        z = z_ref[...]
        z16 = (z + dot16(z.astype(jnp.bfloat16), s_ref[...].astype(jnp.bfloat16))).astype(jnp.bfloat16)
        s_ref[...] = z16.astype(jnp.float32)
        load_residual()
        r = r_ref[...]
        start = dot16(r.astype(jnp.bfloat16), z16).astype(jnp.bfloat16)
        residual = r - (dot16(start, a16_ref[0]) + dot16(start, a16_ref[1]))
        y_ref[...] = start.astype(jnp.float32) + dot16(residual.astype(jnp.bfloat16), z16)
        limit = jnp.max(jnp.abs(r)) * 2e-6

        def refine(carry):
            step, _, before, limit = carry
            y = y_ref[...]
            y_high, y_low = split(y)
            residual = r_ref[...] - (
                dot16(y_high, a16_ref[0]) + (dot16(y_low, a16_ref[0]) + dot16(y_high, a16_ref[1]))
            )
            y_ref[...] = y + dot16(residual.astype(jnp.bfloat16), s_ref[...].astype(jnp.bfloat16))
            return step + 1, before, jnp.max(jnp.abs(residual)), limit

        worst = jnp.max(jnp.abs(residual))
        lax.while_loop(more, refine, (jnp.int32(0), worst, jnp.maximum(worst, 1e-30), limit))
        finish()

    @pl.when(top > 32.0)
    def _():
        def full(x, y):
            return jnp.dot(x, y, precision=HIGHEST, preferred_element_type=jnp.float32)

        z_ref[...] = -second * a_ref[...]
        add_eye(z_ref, first)

        def body(carry):
            rho, extra = carry
            s_ref[...] = -full(a_ref[...], z_ref[...])
            add_eye(s_ref, 1.0)
            z_ref[...] += full(z_ref[...], s_ref[...])
            return rho * rho, jnp.where(rho < 0.01, extra + 1, extra)

        lax.while_loop(lambda carry: carry[1] < 2, body, (rho, jnp.int32(0)))
        load_residual()
        y_ref[...] = full(r_ref[...], z_ref[...])
        size = jnp.max(jnp.abs(r_ref[...]))

        def refine(carry):
            step, _, before, limit = carry
            residual = r_ref[...] - full(y_ref[...], a_ref[...])
            y_ref[...] += full(residual, z_ref[...])
            return step + 1, before, jnp.max(jnp.abs(residual)), limit

        lax.while_loop(more, refine, (jnp.int32(0), size, jnp.maximum(size, 1e-30), size * 2e-6))
        finish()


def solve(gram_packed, targets, values):
    batches, width, per_batch = targets.shape
    n = batches * per_batch
    square = pltpu.VMEM((n, n), jnp.float32)
    wide = pltpu.VMEM((width, n), jnp.float32)
    vmem = pl.BlockSpec(memory_space=pltpu.VMEM)
    out = jax.ShapeDtypeStruct((width, n), jnp.bfloat16)
    return pl.pallas_call(
        solve_kernel,
        out_shape=(out, out),
        in_specs=[vmem, pl.BlockSpec(memory_space=pl.ANY), pl.BlockSpec(memory_space=pl.ANY)],
        out_specs=(vmem, vmem),
        scratch_shapes=[
            square,
            pltpu.VMEM((2, n, n), jnp.bfloat16),
            square,
            square,
            wide,
            wide,
            pltpu.VMEM(targets.shape, targets.dtype),
            pltpu.VMEM(values.shape, values.dtype),
            pltpu.SemaphoreType.DMA((2,)),
        ],
        compiler_params=pltpu.CompilerParams(vmem_limit_bytes=VMEM_LIMIT),
        cost_estimate=pl.CostEstimate(flops=40 * n * n * n, bytes_accessed=4 * 2**20, transcendentals=0),
    )(gram_packed, targets, values)


def contract_first(a, b):
    return lax.dot_general(a, b, (((0,), (0,)), ((), ())), preferred_element_type=jnp.float32)


def piece_start(index):
    return index // 2 * (TALL + SHORT) + index % 2 * TALL


def key_kernel(place_ref, index_ref, table_ref, keys_ref, slice_ref):
    here, n = keys_ref.shape
    col = place_ref[1]
    picked = lax.broadcasted_iota(jnp.int32, (table_ref.shape[1], n), 0) == index_ref[...]
    picked = jnp.where(picked, 1.0, 0.0).astype(jnp.bfloat16)
    keys = dot16(table_ref[...], picked).astype(jnp.bfloat16)
    keys_ref[...] = keys
    padded = slice_ref.shape[0]
    slot = lax.broadcasted_iota(jnp.int32, (padded, here), 0)
    spot = lax.broadcasted_iota(jnp.int32, (padded, here), 1)
    odd = lax.rem(col, 2)
    first = lax.div(col, 2) * (TALL + SHORT) + odd * TALL
    taken = jnp.logical_and(slot + first == spot, slot < TALL - odd * (TALL - SHORT))
    taken = jnp.where(taken, 1.0, 0.0).astype(jnp.bfloat16)
    slice_ref[...] = dot16(taken, keys).astype(jnp.bfloat16)


def select_keys(place, index, table):
    n = index.shape[1]
    vmem = pl.BlockSpec(memory_space=pltpu.VMEM)
    return pl.pallas_call(
        key_kernel,
        out_shape=(
            jax.ShapeDtypeStruct((table.shape[0], n), jnp.bfloat16),
            jax.ShapeDtypeStruct((PADDED, n), jnp.bfloat16),
        ),
        in_specs=[pl.BlockSpec(memory_space=pltpu.SMEM)] + [vmem] * 2,
        out_specs=(vmem, vmem),
        compiler_params=pltpu.CompilerParams(vmem_limit_bytes=VMEM_LIMIT),
    )(place, index, table)


def front_kernel(place_ref, keys_ref, cov_ref, weight_ref, mine_ref, other_ref, part_ref, value_ref):
    here, n = keys_ref.shape
    chips = mine_ref.shape[0]
    share = mine_ref.shape[1] - TALL
    core = place_ref[0]
    keys = keys_ref[...]
    high, low = split(cov_ref[...])
    part_ref[...] = contract_first(high, keys) + contract_first(low, keys)
    value_ref[...] = dot16(weight_ref[...], keys)
    for which, ref in ((core, mine_ref), (1 - core, other_ref)):
        lanes = pl.ds(pl.multiple_of(which * (n // 2), LANES), n // 2)
        for j in range(chips):
            begin = pl.multiple_of(which * here + piece_start(j), 8)
            tall = TALL if j % 2 == 0 else SHORT
            ref[j, :tall, :] = part_ref[pl.ds(begin, tall), :]
            if tall < TALL:
                ref[j, tall:TALL, :] = jnp.zeros((TALL - tall, n), jnp.float32)
            at = j // 2 * (2 * share + V_SHORT) + j % 2 * 2 * share
            second = share if j % 2 == 0 else V_SHORT - share
            ref[j, TALL:, :n // 2] = value_ref[at:at + share, lanes]
            ref[j, TALL:TALL + second, n // 2:] = value_ref[at + share:at + share + second, lanes]
            if second < share:
                ref[j, TALL + second:, n // 2:] = jnp.zeros((share - second, n // 2), jnp.float32)


def front(place, keys, cov, weight, chips):
    n = keys.shape[1]
    width = weight.shape[0]
    share = width // (2 * chips) + 2
    payload = jax.ShapeDtypeStruct((chips, TALL + share, n), jnp.float32)
    vmem = pl.BlockSpec(memory_space=pltpu.VMEM)
    return pl.pallas_call(
        front_kernel,
        out_shape=(payload, payload),
        in_specs=[pl.BlockSpec(memory_space=pltpu.SMEM)] + [vmem] * 3,
        out_specs=(vmem, vmem),
        scratch_shapes=[pltpu.VMEM((cov.shape[1], n), jnp.float32), pltpu.VMEM((width, n), jnp.float32)],
        compiler_params=pltpu.CompilerParams(vmem_limit_bytes=VMEM_LIMIT),
        cost_estimate=pl.CostEstimate(flops=4 * cov.size * n, bytes_accessed=8 * 2**20, transcendentals=0),
    )(place, keys, cov, weight)


def gram_kernel(received_ref, key_ref, panel_ref, value_ref, packed_ref):
    total = received_ref[0]
    for j in range(1, received_ref.shape[0]):
        total = total + received_ref[j]
    panel = total[:TALL]
    panel_ref[...] = panel
    value_ref[...] = total[TALL:]
    n = panel.shape[1]
    padded = jnp.concatenate([panel, jnp.zeros((PADDED - TALL, n), jnp.float32)], axis=0)
    high = padded.astype(jnp.bfloat16)
    rest = padded - high.astype(jnp.float32)
    middle, low = split(rest)
    keys = key_ref[...]
    gram = contract_first(keys, high) + (contract_first(keys, middle) + contract_first(keys, low))
    place = 0
    for i in range(n // LANES):
        for j in range(i + 1):
            packed_ref[place * LANES:(place + 1) * LANES, :] = gram[
                i * LANES:(i + 1) * LANES, j * LANES:(j + 1) * LANES
            ]
            place += 1


def gram_share(received, key_piece):
    n = received.shape[2]
    blocks = n // LANES
    vmem = pl.BlockSpec(memory_space=pltpu.VMEM)
    return pl.pallas_call(
        gram_kernel,
        out_shape=(
            jax.ShapeDtypeStruct((TALL, n), jnp.float32),
            jax.ShapeDtypeStruct((received.shape[1] - TALL, n), jnp.float32),
            jax.ShapeDtypeStruct((blocks * (blocks + 1) // 2 * LANES, LANES), jnp.float32),
        ),
        in_specs=[vmem] * 2,
        out_specs=(vmem, vmem, vmem),
        compiler_params=pltpu.CompilerParams(vmem_limit_bytes=VMEM_LIMIT),
    )(received, key_piece)


def change_kernel(place_ref, *refs):
    *bundle_refs, high_ref, low_ref, out_ref, panel_ref = refs
    cols = len(bundle_refs) * STRIDE
    for shift, ref in zip(SHIFTS, bundle_refs):
        for t in range(cols // STRIDE):
            piece = lax.rem(place_ref[1] - shift - STRIDE * t + 2 * cols, cols)
            odd = lax.rem(piece, 2)
            begin = pl.multiple_of(lax.div(piece, 2) * (TALL + SHORT) + odd * TALL, 8)
            panel_ref[pl.ds(begin, SHORT), :] = ref[t * TALL:t * TALL + SHORT, :]

            @pl.when(odd == 0)
            def _(ref=ref, t=t, begin=begin):
                panel_ref[pl.ds(begin + SHORT, TALL - SHORT), :] = ref[t * TALL + SHORT:(t + 1) * TALL, :]

    high, low = split(panel_ref[...])
    last = (((1,), (1,)), ((), ()))
    out = lax.dot_general(high_ref[...], high, last, preferred_element_type=jnp.float32)
    out += lax.dot_general(low_ref[...], high, last, preferred_element_type=jnp.float32)
    out += lax.dot_general(high_ref[...], low, last, preferred_element_type=jnp.float32)
    out_ref[...] = out.astype(jnp.bfloat16)


def change(place, bundles, solved, here):
    width, n = solved[0].shape
    vmem = pl.BlockSpec(memory_space=pltpu.VMEM)
    return pl.pallas_call(
        change_kernel,
        out_shape=jax.ShapeDtypeStruct((width, here), jnp.bfloat16),
        in_specs=[pl.BlockSpec(memory_space=pltpu.SMEM)] + [vmem] * (len(bundles) + 2),
        out_specs=vmem,
        scratch_shapes=[pltpu.VMEM((here, n), jnp.float32)],
        compiler_params=pltpu.CompilerParams(vmem_limit_bytes=VMEM_LIMIT),
    )(place, *bundles, *solved)


def moved(value, axis, shift):
    size = lax.axis_size(axis)
    return lax.ppermute(value, axis, [(i, (i + shift) % size) for i in range(size)])


def swapped(value, axis, groups=None):
    return lax.all_to_all(value, axis, 0, 0, axis_index_groups=groups, tiled=True)


def copies(value, count):
    return jnp.broadcast_to(value, (count, *value.shape))


def shards(inverse_cov, key_table, weight, edit_index, targets):
    rows = lax.axis_size("row")
    cols = lax.axis_size("col")
    chips = rows // 2
    here = inverse_cov.shape[0]
    n = edit_index.size
    place = jnp.stack([lax.axis_index("row") % 2, lax.axis_index("col")]).astype(jnp.int32)
    turned = [((2 * a + h) * cols + b, (2 * b + h) * cols + a) for a in range(chips) for b in range(cols) for h in range(2)]
    same_core = [[2 * k + h for k in range(chips)] for h in range(2)]
    other_core = [(r, r ^ 1) for r in range(rows)]

    keys, key_slice = select_keys(place, edit_index.reshape(1, n), key_table.T)
    key_piece = lax.ppermute(key_slice, ("row", "col"), turned)
    mine, other = front(place, keys, inverse_cov, weight.T, chips)
    half_sum = mine + lax.ppermute(other, "row", other_core)
    received = swapped(half_sum, "row", same_core)
    panel_piece, value_piece, packed = gram_share(received, key_piece)
    near = lax.ppermute(panel_piece, ("row", "col"), turned)
    share = packed.shape[0] // rows
    neighbours = [[STRIDE * g + i for i in range(STRIDE)] for g in range(cols // STRIDE)]
    part = jnp.sum(swapped(packed.reshape(rows, share, LANES), "row"), axis=0)
    part, near = lax.optimization_barrier((part, near))
    part = jnp.sum(swapped(copies(part, STRIDE), "col", neighbours), axis=0)
    part, value_piece = lax.optimization_barrier((part, value_piece))
    values = swapped(copies(value_piece, rows), "row")
    part = part + sum(moved(part, "col", STRIDE * t) for t in range(1, cols // STRIDE))
    part, near, values = lax.optimization_barrier((part, near, values))
    far = [near] + [moved(near, "col", STRIDE * t) for t in range(1, cols // STRIDE)]
    gram = swapped(copies(part, rows), "row")
    gram, *far = lax.optimization_barrier((gram, *far))
    far = jnp.concatenate(far, axis=0)
    bundles = [far] + [moved(far, "col", shift) for shift in SHIFTS[1:]]
    solved = solve(gram.reshape(rows * share, LANES), jnp.swapaxes(targets, 1, 2), values)
    return change(place, bundles, solved, here).T


def solution(mesh):
    in_specs = (P("row", "col"), P(None, "row"), P("row", "col"), P(), P(None, None, "col"))
    out_specs = P("row", "col")
    return jax.shard_map(shards, mesh=mesh, in_specs=in_specs, out_specs=out_specs, check_vma=False)
```

```python
import math

import jax
import jax.numpy as jnp
from jax import lax
from jax.experimental import pallas as pl
from jax.experimental.pallas import tpu as pltpu
from jax.sharding import PartitionSpec as P

F = 18432
LANES = 128
HIGHEST = lax.Precision.HIGHEST
VMEM_LIMIT = 48 * 2**20
TALL, SHORT, PADDED = 40, 32, 48
V_SHORT = 24
STRIDE = 4
SHIFTS = (0, 1, 2, -1)


def split(value):
    high = value.astype(jnp.bfloat16)
    return high, (value - high.astype(jnp.float32)).astype(jnp.bfloat16)


def dot16(a, b):
    return jnp.dot(a, b, preferred_element_type=jnp.float32)


def solve_kernel(gram_ref, target_hbm, value_hbm, high_out, low_out, a_ref, a16_ref, z_ref, s_ref, r_ref, y_ref, target_ref, value_ref, sems):
    n = a_ref.shape[0]
    width = r_ref.shape[0]
    target_copy = pltpu.make_async_copy(target_hbm, target_ref, sems.at[0])
    value_copy = pltpu.make_async_copy(value_hbm, value_ref, sems.at[1])
    target_copy.start()
    value_copy.start()
    blocks = n // LANES
    rows = lax.broadcasted_iota(jnp.int32, (LANES, LANES), 0)
    cols = lax.broadcasted_iota(jnp.int32, (LANES, LANES), 1)
    eye = jnp.where(rows == cols, 1.0, 0.0).astype(jnp.float32)
    place = 0
    for i in range(blocks):
        for j in range(i + 1):
            block = gram_ref[place * LANES:(place + 1) * LANES, :]
            place += 1
            if i == j:
                a_ref[i * LANES:(i + 1) * LANES, j * LANES:(j + 1) * LANES] = block + eye
            else:
                a_ref[i * LANES:(i + 1) * LANES, j * LANES:(j + 1) * LANES] = block
                a_ref[j * LANES:(j + 1) * LANES, i * LANES:(i + 1) * LANES] = block.T
    a = a_ref[...]
    top = jnp.maximum(jnp.max(jnp.sum(jnp.abs(a), axis=0)), 1.0)
    high = a.astype(jnp.bfloat16)
    a16_ref[0] = high
    a16_ref[1] = (a - high.astype(jnp.float32)).astype(jnp.bfloat16)
    middle = top + 1.0
    span = top - 1.0
    scale = 2.0 * middle * middle - span * span
    first, second = 8.0 * middle / scale, 8.0 / scale
    rho = span * span / scale

    def add_eye(ref, times):
        for i in range(blocks):
            at = slice(i * LANES, (i + 1) * LANES)
            ref[at, at] += eye * times

    def load_residual():
        target_copy.wait()
        value_copy.wait()
        per_batch = target_ref.shape[2]
        share = value_ref.shape[1]
        for b in range(target_ref.shape[0]):
            r_ref[:, b * per_batch:(b + 1) * per_batch] = target_ref[b].astype(jnp.float32)
        half = n // 2
        for r in range(value_ref.shape[0]):
            k, h = r // 2, r % 2
            tall = 2 * share if k % 2 == 0 else V_SHORT
            begin = k // 2 * (2 * share + V_SHORT) + k % 2 * 2 * share
            at = slice(h * half, (h + 1) * half)
            r_ref[begin:begin + share, at] -= value_ref[r, :, :half]
            r_ref[begin + share:begin + tall, at] -= value_ref[r, :tall - share, half:]

    def more(carry):
        step, before, worst, limit = carry
        return jnp.logical_and(step < 12, worst * worst > limit * before)

    def finish():
        result = y_ref[...] * math.sqrt(F)
        high, low = split(result)
        high_out[...] = high
        low_out[...] = low

    @pl.when(top <= 32.0)
    def _():
        z_ref[...] = -second * a_ref[...]
        add_eye(z_ref, first)
        s_ref[...] = second * dot16(a16_ref[0], a16_ref[0]) - first * a_ref[...]
        add_eye(s_ref, 1.0)

        def body(rho):
            s16 = s_ref[...].astype(jnp.bfloat16)
            both = dot16(jnp.concatenate([z_ref[...].astype(jnp.bfloat16), s16], axis=0), s16)
            z_ref[...] += both[:n]
            s_ref[...] = both[n:]
            return rho * rho

        lax.while_loop(lambda rho: rho * rho > 0.004, body, rho)
        z = z_ref[...]
        z16 = (z + dot16(z.astype(jnp.bfloat16), s_ref[...].astype(jnp.bfloat16))).astype(jnp.bfloat16)
        s_ref[...] = z16.astype(jnp.float32)
        load_residual()
        r = r_ref[...]
        start = dot16(r.astype(jnp.bfloat16), z16).astype(jnp.bfloat16)
        residual = r - (dot16(start, a16_ref[0]) + dot16(start, a16_ref[1]))
        y_ref[...] = start.astype(jnp.float32) + dot16(residual.astype(jnp.bfloat16), z16)
        limit = jnp.max(jnp.abs(r)) * 2e-6

        def refine(carry):
            step, _, before, limit = carry
            y = y_ref[...]
            y_high, y_low = split(y)
            residual = r_ref[...] - (
                dot16(y_high, a16_ref[0]) + (dot16(y_low, a16_ref[0]) + dot16(y_high, a16_ref[1]))
            )
            y_ref[...] = y + dot16(residual.astype(jnp.bfloat16), s_ref[...].astype(jnp.bfloat16))
            return step + 1, before, jnp.max(jnp.abs(residual)), limit

        worst = jnp.max(jnp.abs(residual))
        lax.while_loop(more, refine, (jnp.int32(0), worst, jnp.maximum(worst, 1e-30), limit))
        finish()

    @pl.when(top > 32.0)
    def _():
        def full(x, y):
            return jnp.dot(x, y, precision=HIGHEST, preferred_element_type=jnp.float32)

        z_ref[...] = -second * a_ref[...]
        add_eye(z_ref, first)

        def body(carry):
            rho, extra = carry
            s_ref[...] = -full(a_ref[...], z_ref[...])
            add_eye(s_ref, 1.0)
            z_ref[...] += full(z_ref[...], s_ref[...])
            return rho * rho, jnp.where(rho < 0.01, extra + 1, extra)

        lax.while_loop(lambda carry: carry[1] < 2, body, (rho, jnp.int32(0)))
        load_residual()
        y_ref[...] = full(r_ref[...], z_ref[...])
        size = jnp.max(jnp.abs(r_ref[...]))

        def refine(carry):
            step, _, before, limit = carry
            residual = r_ref[...] - full(y_ref[...], a_ref[...])
            y_ref[...] += full(residual, z_ref[...])
            return step + 1, before, jnp.max(jnp.abs(residual)), limit

        lax.while_loop(more, refine, (jnp.int32(0), size, jnp.maximum(size, 1e-30), size * 2e-6))
        finish()


def solve(gram_packed, targets, values):
    batches, width, per_batch = targets.shape
    n = batches * per_batch
    square = pltpu.VMEM((n, n), jnp.float32)
    wide = pltpu.VMEM((width, n), jnp.float32)
    vmem = pl.BlockSpec(memory_space=pltpu.VMEM)
    out = jax.ShapeDtypeStruct((width, n), jnp.bfloat16)
    return pl.pallas_call(
        solve_kernel,
        out_shape=(out, out),
        in_specs=[vmem, pl.BlockSpec(memory_space=pl.ANY), pl.BlockSpec(memory_space=pl.ANY)],
        out_specs=(vmem, vmem),
        scratch_shapes=[
            square,
            pltpu.VMEM((2, n, n), jnp.bfloat16),
            square,
            square,
            wide,
            wide,
            pltpu.VMEM(targets.shape, targets.dtype),
            pltpu.VMEM(values.shape, values.dtype),
            pltpu.SemaphoreType.DMA((2,)),
        ],
        compiler_params=pltpu.CompilerParams(vmem_limit_bytes=VMEM_LIMIT),
        cost_estimate=pl.CostEstimate(flops=40 * n * n * n, bytes_accessed=4 * 2**20, transcendentals=0),
    )(gram_packed, targets, values)


def contract_first(a, b):
    return lax.dot_general(a, b, (((0,), (0,)), ((), ())), preferred_element_type=jnp.float32)


def piece_start(index):
    return index // 2 * (TALL + SHORT) + index % 2 * TALL


def front_kernel(place_ref, index_ref, table_hbm, cov_hbm, weight_hbm, other_ref, mine_ref, slice_ref, table_ref, cov_ref, weight_ref, part_ref, value_ref, sems):
    loads = [
        pltpu.make_async_copy(src, dst, sems.at[i])
        for i, (src, dst) in enumerate(((table_hbm, table_ref), (cov_hbm, cov_ref), (weight_hbm, weight_ref)))
    ]
    for load in loads:
        load.start()
    here, n = table_ref.shape[0], slice_ref.shape[1]
    chips = mine_ref.shape[0]
    share = mine_ref.shape[1] - TALL
    core, col = place_ref[0], place_ref[1]
    batches, per_batch = index_ref.shape
    spot = lax.broadcasted_iota(jnp.int32, (table_ref.shape[1], per_batch), 0)
    picked = jnp.concatenate(
        [jnp.where(spot == index_ref[b:b + 1, :], 1.0, 0.0).astype(jnp.bfloat16) for b in range(batches)], axis=1
    )
    loads[0].wait()
    keys = dot16(table_ref[...], picked).astype(jnp.bfloat16)
    padded = slice_ref.shape[0]
    slot = lax.broadcasted_iota(jnp.int32, (padded, here), 0)
    spot = lax.broadcasted_iota(jnp.int32, (padded, here), 1)
    odd = lax.rem(col, 2)
    first = lax.div(col, 2) * (TALL + SHORT) + odd * TALL
    taken = jnp.logical_and(slot + first == spot, slot < TALL - odd * (TALL - SHORT))
    taken = jnp.where(taken, 1.0, 0.0).astype(jnp.bfloat16)
    slice_ref[...] = dot16(taken, keys).astype(jnp.bfloat16)
    loads[2].wait()
    value_ref[...] = dot16(weight_ref[...], keys)
    loads[1].wait()
    high, low = split(cov_ref[...])
    part_ref[...] = contract_first(high, keys) + contract_first(low, keys)
    for which, ref in ((core, mine_ref), (1 - core, other_ref)):
        lanes = pl.ds(pl.multiple_of(which * (n // 2), LANES), n // 2)
        for j in range(chips):
            begin = pl.multiple_of(which * here + piece_start(j), 8)
            tall = TALL if j % 2 == 0 else SHORT
            ref[j, :tall, :] = part_ref[pl.ds(begin, tall), :]
            if tall < TALL:
                ref[j, tall:TALL, :] = jnp.zeros((TALL - tall, n), jnp.float32)
            at = j // 2 * (2 * share + V_SHORT) + j % 2 * 2 * share
            second = share if j % 2 == 0 else V_SHORT - share
            ref[j, TALL:, :n // 2] = value_ref[at:at + share, lanes]
            ref[j, TALL:TALL + second, n // 2:] = value_ref[at + share:at + share + second, lanes]
            if second < share:
                ref[j, TALL + second:, n // 2:] = jnp.zeros((share - second, n // 2), jnp.float32)


def front(place, index, table, cov, weight, chips):
    n = index.size
    width = weight.shape[0]
    share = width // (2 * chips) + 2
    payload = jax.ShapeDtypeStruct((chips, TALL + share, n), jnp.float32)
    vmem = pl.BlockSpec(memory_space=pltpu.VMEM)
    return pl.pallas_call(
        front_kernel,
        out_shape=(payload, payload, jax.ShapeDtypeStruct((PADDED, n), jnp.bfloat16)),
        in_specs=[pl.BlockSpec(memory_space=pltpu.SMEM), vmem] + [pl.BlockSpec(memory_space=pl.ANY)] * 3,
        out_specs=(vmem, vmem, vmem),
        scratch_shapes=[
            pltpu.VMEM(table.shape, table.dtype),
            pltpu.VMEM(cov.shape, cov.dtype),
            pltpu.VMEM(weight.shape, weight.dtype),
            pltpu.VMEM((cov.shape[1], n), jnp.float32),
            pltpu.VMEM((width, n), jnp.float32),
            pltpu.SemaphoreType.DMA((3,)),
        ],
        compiler_params=pltpu.CompilerParams(vmem_limit_bytes=60 * 2**20),
    )(place, index, table, cov, weight)


def gram_kernel(panel_ref, key_ref, packed_ref):
    panel = panel_ref[...]
    n = panel.shape[1]
    padded = jnp.concatenate([panel, jnp.zeros((PADDED - TALL, n), jnp.float32)], axis=0)
    high = padded.astype(jnp.bfloat16)
    rest = padded - high.astype(jnp.float32)
    middle, low = split(rest)
    keys = key_ref[...]
    gram = contract_first(keys, high) + (contract_first(keys, middle) + contract_first(keys, low))
    place = 0
    for i in range(n // LANES):
        for j in range(i + 1):
            packed_ref[place * LANES:(place + 1) * LANES, :] = gram[
                i * LANES:(i + 1) * LANES, j * LANES:(j + 1) * LANES
            ]
            place += 1


def gram_share(panel, key_piece):
    blocks = panel.shape[1] // LANES
    vmem = pl.BlockSpec(memory_space=pltpu.VMEM)
    return pl.pallas_call(
        gram_kernel,
        out_shape=jax.ShapeDtypeStruct((blocks * (blocks + 1) // 2 * LANES, LANES), jnp.float32),
        in_specs=[vmem] * 2,
        out_specs=vmem,
        compiler_params=pltpu.CompilerParams(vmem_limit_bytes=VMEM_LIMIT),
    )(panel, key_piece)


def change_kernel(place_ref, *refs):
    *bundle_refs, high_ref, low_ref, out_ref, panel_ref = refs
    cols = len(bundle_refs) * STRIDE
    for shift, ref in zip(SHIFTS, bundle_refs):
        for t in range(cols // STRIDE):
            piece = lax.rem(place_ref[1] - shift - STRIDE * t + 2 * cols, cols)
            odd = lax.rem(piece, 2)
            begin = pl.multiple_of(lax.div(piece, 2) * (TALL + SHORT) + odd * TALL, 8)
            panel_ref[pl.ds(begin, SHORT), :] = ref[t * TALL:t * TALL + SHORT, :]

            @pl.when(odd == 0)
            def _(ref=ref, t=t, begin=begin):
                panel_ref[pl.ds(begin + SHORT, TALL - SHORT), :] = ref[t * TALL + SHORT:(t + 1) * TALL, :]

    high, low = split(panel_ref[...])
    last = (((1,), (1,)), ((), ()))
    out = lax.dot_general(high_ref[...], high, last, preferred_element_type=jnp.float32)
    out += lax.dot_general(low_ref[...], high, last, preferred_element_type=jnp.float32)
    out += lax.dot_general(high_ref[...], low, last, preferred_element_type=jnp.float32)
    out_ref[...] = out.astype(jnp.bfloat16)


def change(place, bundles, solved, here):
    width, n = solved[0].shape
    vmem = pl.BlockSpec(memory_space=pltpu.VMEM)
    return pl.pallas_call(
        change_kernel,
        out_shape=jax.ShapeDtypeStruct((width, here), jnp.bfloat16),
        in_specs=[pl.BlockSpec(memory_space=pltpu.SMEM)] + [vmem] * (len(bundles) + 2),
        out_specs=vmem,
        scratch_shapes=[pltpu.VMEM((here, n), jnp.float32)],
        compiler_params=pltpu.CompilerParams(vmem_limit_bytes=VMEM_LIMIT),
    )(place, *bundles, *solved)


def moved(value, axis, shift):
    size = lax.axis_size(axis)
    return lax.ppermute(value, axis, [(i, (i + shift) % size) for i in range(size)])


def swapped(value, axis, groups=None):
    return lax.all_to_all(value, axis, 0, 0, axis_index_groups=groups, tiled=True)


def copies(value, count):
    return jnp.broadcast_to(value, (count, *value.shape))


def shards(inverse_cov, key_table, weight, edit_index, targets):
    rows = lax.axis_size("row")
    cols = lax.axis_size("col")
    chips = rows // 2
    here = inverse_cov.shape[0]
    n = edit_index.size
    place = jnp.stack([lax.axis_index("row") % 2, lax.axis_index("col")]).astype(jnp.int32)
    turned = [((2 * a + h) * cols + b, (2 * b + h) * cols + a) for a in range(chips) for b in range(cols) for h in range(2)]
    same_core = [[2 * k + h for k in range(chips)] for h in range(2)]
    other_core = [(r, r ^ 1) for r in range(rows)]

    other, mine, key_piece = front(place, edit_index, key_table.T, inverse_cov, weight.T, chips)
    half_sum = mine + lax.ppermute(other, "row", other_core)
    panel_piece = jnp.sum(swapped(half_sum[:, :TALL], "row", same_core), axis=0)
    own = lax.ppermute(panel_piece, ("row", "col"), turned)
    value_parts, _ = lax.optimization_barrier((half_sum[:, TALL:], panel_piece))
    value_piece = jnp.sum(swapped(value_parts, "row", same_core), axis=0)
    own, value_piece = lax.optimization_barrier((own, value_piece))
    packed = gram_share(own, key_piece)

    neighbours = [[STRIDE * g + i for i in range(STRIDE)] for g in range(cols // STRIDE)]
    share = packed.shape[0] // rows
    far = [own] + [moved(own, "col", STRIDE * t) for t in range(1, cols // STRIDE)]
    part = jnp.sum(swapped(packed.reshape(rows, share, LANES), "row"), axis=0)
    part, *far = lax.optimization_barrier((part, *far))
    part = jnp.sum(swapped(copies(part, STRIDE), "col", neighbours), axis=0)
    part, value_piece = lax.optimization_barrier((part, value_piece))
    values = swapped(copies(value_piece, rows), "row")
    part = part + sum(moved(part, "col", STRIDE * t) for t in range(1, cols // STRIDE))
    part, values, *far = lax.optimization_barrier((part, values, *far))
    gram = swapped(copies(part, rows), "row")
    far = jnp.concatenate(far, axis=0)
    bundles = [far] + [moved(far, "col", shift) for shift in SHIFTS[1:]]
    solved = solve(gram.reshape(rows * share, LANES), jnp.swapaxes(targets, 1, 2), values)
    return change(place, bundles, solved, here).T


def solution(mesh):
    in_specs = (P("row", "col"), P(None, "row"), P("row", "col"), P(), P(None, None, "col"))
    out_specs = P("row", "col")
    return jax.shard_map(shards, mesh=mesh, in_specs=in_specs, out_specs=out_specs, check_vma=False)
```

```python
import math

import jax
import jax.numpy as jnp
from jax import lax
from jax.experimental import pallas as pl
from jax.experimental.pallas import tpu as pltpu
from jax.sharding import PartitionSpec as P

F = 18432
LANES = 128
HIGHEST = lax.Precision.HIGHEST
VMEM_LIMIT = 48 * 2**20
TALL, SHORT, PADDED = 40, 32, 48
V_SHORT = 24
STRIDE = 4
SHIFTS = (0, 1, 2, -1)


def split(value):
    high = value.astype(jnp.bfloat16)
    return high, (value - high.astype(jnp.float32)).astype(jnp.bfloat16)


def dot16(a, b):
    return jnp.dot(a, b, preferred_element_type=jnp.float32)


def solve_kernel(gram_ref, target_hbm, value_hbm, high_out, low_out, a_ref, a16_ref, z_ref, s_ref, r_ref, y_ref, target_ref, value_ref, sems):
    n = a_ref.shape[0]
    width = r_ref.shape[0]
    target_copy = pltpu.make_async_copy(target_hbm, target_ref, sems.at[0])
    value_copy = pltpu.make_async_copy(value_hbm, value_ref, sems.at[1])
    target_copy.start()
    value_copy.start()
    blocks = n // LANES
    rows = lax.broadcasted_iota(jnp.int32, (LANES, LANES), 0)
    cols = lax.broadcasted_iota(jnp.int32, (LANES, LANES), 1)
    eye = jnp.where(rows == cols, 1.0, 0.0).astype(jnp.float32)
    place = 0
    for i in range(blocks):
        for j in range(i + 1):
            block = gram_ref[place * LANES:(place + 1) * LANES, :]
            place += 1
            if i == j:
                a_ref[i * LANES:(i + 1) * LANES, j * LANES:(j + 1) * LANES] = block + eye
            else:
                a_ref[i * LANES:(i + 1) * LANES, j * LANES:(j + 1) * LANES] = block
                a_ref[j * LANES:(j + 1) * LANES, i * LANES:(i + 1) * LANES] = block.T
    a = a_ref[...]
    top = jnp.maximum(jnp.max(jnp.sum(jnp.abs(a), axis=0)), 1.0)
    high = a.astype(jnp.bfloat16)
    a16_ref[0] = high
    a16_ref[1] = (a - high.astype(jnp.float32)).astype(jnp.bfloat16)
    middle = top + 1.0
    span = top - 1.0
    scale = 2.0 * middle * middle - span * span
    first, second = 8.0 * middle / scale, 8.0 / scale
    rho = span * span / scale

    def add_eye(ref, times):
        for i in range(blocks):
            at = slice(i * LANES, (i + 1) * LANES)
            ref[at, at] += eye * times

    def load_residual():
        target_copy.wait()
        value_copy.wait()
        per_batch = target_ref.shape[2]
        share = value_ref.shape[1]
        for b in range(target_ref.shape[0]):
            r_ref[:, b * per_batch:(b + 1) * per_batch] = target_ref[b].astype(jnp.float32)
        half = n // 2
        for r in range(value_ref.shape[0]):
            k, h = r // 2, r % 2
            tall = 2 * share if k % 2 == 0 else V_SHORT
            begin = k // 2 * (2 * share + V_SHORT) + k % 2 * 2 * share
            at = slice(h * half, (h + 1) * half)
            r_ref[begin:begin + share, at] -= value_ref[r, :, :half]
            r_ref[begin + share:begin + tall, at] -= value_ref[r, :tall - share, half:]

    def more(carry):
        step, before, worst, limit = carry
        return jnp.logical_and(step < 12, worst * worst > limit * before)

    def finish():
        result = y_ref[...] * math.sqrt(F)
        high, low = split(result)
        high_out[...] = high
        low_out[...] = low

    @pl.when(top <= 32.0)
    def _():
        z_ref[...] = -second * a_ref[...]
        add_eye(z_ref, first)
        s_ref[...] = second * dot16(a16_ref[0], a16_ref[0]) - first * a_ref[...]
        add_eye(s_ref, 1.0)

        def body(rho):
            s16 = s_ref[...].astype(jnp.bfloat16)
            both = dot16(jnp.concatenate([z_ref[...].astype(jnp.bfloat16), s16], axis=0), s16)
            z_ref[...] += both[:n]
            s_ref[...] = both[n:]
            return rho * rho

        lax.while_loop(lambda rho: rho * rho > 0.004, body, rho)
        z = z_ref[...]
        z16 = (z + dot16(z.astype(jnp.bfloat16), s_ref[...].astype(jnp.bfloat16))).astype(jnp.bfloat16)
        s_ref[...] = z16.astype(jnp.float32)
        load_residual()
        r = r_ref[...]
        start = dot16(r.astype(jnp.bfloat16), z16).astype(jnp.bfloat16)
        residual = r - (dot16(start, a16_ref[0]) + dot16(start, a16_ref[1]))
        y_ref[...] = start.astype(jnp.float32) + dot16(residual.astype(jnp.bfloat16), z16)
        limit = jnp.max(jnp.abs(r)) * 2e-6

        def refine(carry):
            step, _, before, limit = carry
            y = y_ref[...]
            y_high, y_low = split(y)
            residual = r_ref[...] - (
                dot16(y_high, a16_ref[0]) + (dot16(y_low, a16_ref[0]) + dot16(y_high, a16_ref[1]))
            )
            y_ref[...] = y + dot16(residual.astype(jnp.bfloat16), s_ref[...].astype(jnp.bfloat16))
            return step + 1, before, jnp.max(jnp.abs(residual)), limit

        worst = jnp.max(jnp.abs(residual))
        lax.while_loop(more, refine, (jnp.int32(0), worst, jnp.maximum(worst, 1e-30), limit))
        finish()

    @pl.when(top > 32.0)
    def _():
        def full(x, y):
            return jnp.dot(x, y, precision=HIGHEST, preferred_element_type=jnp.float32)

        z_ref[...] = -second * a_ref[...]
        add_eye(z_ref, first)

        def body(carry):
            rho, extra = carry
            s_ref[...] = -full(a_ref[...], z_ref[...])
            add_eye(s_ref, 1.0)
            z_ref[...] += full(z_ref[...], s_ref[...])
            return rho * rho, jnp.where(rho < 0.01, extra + 1, extra)

        lax.while_loop(lambda carry: carry[1] < 2, body, (rho, jnp.int32(0)))
        load_residual()
        y_ref[...] = full(r_ref[...], z_ref[...])
        size = jnp.max(jnp.abs(r_ref[...]))

        def refine(carry):
            step, _, before, limit = carry
            residual = r_ref[...] - full(y_ref[...], a_ref[...])
            y_ref[...] += full(residual, z_ref[...])
            return step + 1, before, jnp.max(jnp.abs(residual)), limit

        lax.while_loop(more, refine, (jnp.int32(0), size, jnp.maximum(size, 1e-30), size * 2e-6))
        finish()


def solve(gram_packed, targets, values):
    batches, width, per_batch = targets.shape
    n = batches * per_batch
    square = pltpu.VMEM((n, n), jnp.float32)
    wide = pltpu.VMEM((width, n), jnp.float32)
    vmem = pl.BlockSpec(memory_space=pltpu.VMEM)
    out = jax.ShapeDtypeStruct((width, n), jnp.bfloat16)
    return pl.pallas_call(
        solve_kernel,
        out_shape=(out, out),
        in_specs=[vmem, pl.BlockSpec(memory_space=pl.ANY), pl.BlockSpec(memory_space=pl.ANY)],
        out_specs=(vmem, vmem),
        scratch_shapes=[
            square,
            pltpu.VMEM((2, n, n), jnp.bfloat16),
            square,
            square,
            wide,
            wide,
            pltpu.VMEM(targets.shape, targets.dtype),
            pltpu.VMEM(values.shape, values.dtype),
            pltpu.SemaphoreType.DMA((2,)),
        ],
        compiler_params=pltpu.CompilerParams(vmem_limit_bytes=VMEM_LIMIT),
        cost_estimate=pl.CostEstimate(flops=40 * n * n * n, bytes_accessed=4 * 2**20, transcendentals=0),
    )(gram_packed, targets, values)


def contract_first(a, b):
    return lax.dot_general(a, b, (((0,), (0,)), ((), ())), preferred_element_type=jnp.float32)


def piece_start(index):
    return index // 2 * (TALL + SHORT) + index % 2 * TALL


def front_kernel(place_ref, index_ref, table_hbm, cov_hbm, weight_hbm, other_ref, mine_ref, slice_ref, table_ref, cov_ref, weight_ref, part_ref, value_ref, sems):
    loads = [
        pltpu.make_async_copy(src, dst, sems.at[i])
        for i, (src, dst) in enumerate(((table_hbm, table_ref), (cov_hbm, cov_ref), (weight_hbm, weight_ref)))
    ]
    for load in loads:
        load.start()
    here, n = table_ref.shape[0], slice_ref.shape[1]
    chips = mine_ref.shape[0]
    share = mine_ref.shape[1] - TALL
    core, col = place_ref[0], place_ref[1]
    batches, per_batch = index_ref.shape
    spot = lax.broadcasted_iota(jnp.int32, (table_ref.shape[1], per_batch), 0)
    picked = jnp.concatenate(
        [jnp.where(spot == index_ref[b:b + 1, :], 1.0, 0.0).astype(jnp.bfloat16) for b in range(batches)], axis=1
    )
    loads[0].wait()
    keys = dot16(table_ref[...], picked).astype(jnp.bfloat16)
    padded = slice_ref.shape[0]
    slot = lax.broadcasted_iota(jnp.int32, (padded, here), 0)
    spot = lax.broadcasted_iota(jnp.int32, (padded, here), 1)
    odd = lax.rem(col, 2)
    first = lax.div(col, 2) * (TALL + SHORT) + odd * TALL
    taken = jnp.logical_and(slot + first == spot, slot < TALL - odd * (TALL - SHORT))
    taken = jnp.where(taken, 1.0, 0.0).astype(jnp.bfloat16)
    slice_ref[...] = dot16(taken, keys).astype(jnp.bfloat16)
    loads[2].wait()
    value_ref[...] = dot16(weight_ref[...], keys)
    loads[1].wait()
    high, low = split(cov_ref[...])
    part_ref[...] = contract_first(high, keys) + contract_first(low, keys)
    for which, ref in ((core, mine_ref), (1 - core, other_ref)):
        lanes = pl.ds(pl.multiple_of(which * (n // 2), LANES), n // 2)
        for j in range(chips):
            begin = pl.multiple_of(which * here + piece_start(j), 8)
            tall = TALL if j % 2 == 0 else SHORT
            ref[j, :tall, :] = part_ref[pl.ds(begin, tall), :]
            if tall < TALL:
                ref[j, tall:TALL, :] = jnp.zeros((TALL - tall, n), jnp.float32)
            at = j // 2 * (2 * share + V_SHORT) + j % 2 * 2 * share
            second = share if j % 2 == 0 else V_SHORT - share
            ref[j, TALL:, :n // 2] = value_ref[at:at + share, lanes]
            ref[j, TALL:TALL + second, n // 2:] = value_ref[at + share:at + share + second, lanes]
            if second < share:
                ref[j, TALL + second:, n // 2:] = jnp.zeros((share - second, n // 2), jnp.float32)


def front(place, index, table, cov, weight, chips):
    n = index.size
    width = weight.shape[0]
    share = width // (2 * chips) + 2
    payload = jax.ShapeDtypeStruct((chips, TALL + share, n), jnp.float32)
    vmem = pl.BlockSpec(memory_space=pltpu.VMEM)
    return pl.pallas_call(
        front_kernel,
        out_shape=(payload, payload, jax.ShapeDtypeStruct((PADDED, n), jnp.bfloat16)),
        in_specs=[pl.BlockSpec(memory_space=pltpu.SMEM), vmem] + [pl.BlockSpec(memory_space=pl.ANY)] * 3,
        out_specs=(vmem, vmem, vmem),
        scratch_shapes=[
            pltpu.VMEM(table.shape, table.dtype),
            pltpu.VMEM(cov.shape, cov.dtype),
            pltpu.VMEM(weight.shape, weight.dtype),
            pltpu.VMEM((cov.shape[1], n), jnp.float32),
            pltpu.VMEM((width, n), jnp.float32),
            pltpu.SemaphoreType.DMA((3,)),
        ],
        compiler_params=pltpu.CompilerParams(vmem_limit_bytes=60 * 2**20),
    )(place, index, table, cov, weight)


def gram_kernel(received_ref, key_ref, panel_ref, value_ref, packed_ref):
    total = received_ref[0]
    for j in range(1, received_ref.shape[0]):
        total = total + received_ref[j]
    panel = total[:TALL]
    panel_ref[...] = panel
    value_ref[...] = total[TALL:]
    n = panel.shape[1]
    padded = jnp.concatenate([panel, jnp.zeros((PADDED - TALL, n), jnp.float32)], axis=0)
    high = padded.astype(jnp.bfloat16)
    rest = padded - high.astype(jnp.float32)
    middle, low = split(rest)
    keys = key_ref[...]
    gram = contract_first(keys, high) + (contract_first(keys, middle) + contract_first(keys, low))
    place = 0
    for i in range(n // LANES):
        for j in range(i + 1):
            packed_ref[place * LANES:(place + 1) * LANES, :] = gram[
                i * LANES:(i + 1) * LANES, j * LANES:(j + 1) * LANES
            ]
            place += 1


def gram_share(received, key_piece):
    n = received.shape[2]
    blocks = n // LANES
    vmem = pl.BlockSpec(memory_space=pltpu.VMEM)
    return pl.pallas_call(
        gram_kernel,
        out_shape=(
            jax.ShapeDtypeStruct((TALL, n), jnp.float32),
            jax.ShapeDtypeStruct((received.shape[1] - TALL, n), jnp.float32),
            jax.ShapeDtypeStruct((blocks * (blocks + 1) // 2 * LANES, LANES), jnp.float32),
        ),
        in_specs=[vmem] * 2,
        out_specs=(vmem, vmem, vmem),
        compiler_params=pltpu.CompilerParams(vmem_limit_bytes=VMEM_LIMIT),
    )(received, key_piece)


def change_kernel(place_ref, *refs):
    *bundle_refs, high_ref, low_ref, out_ref, panel_ref = refs
    cols = len(bundle_refs) * STRIDE
    for shift, ref in zip(SHIFTS, bundle_refs):
        for t in range(cols // STRIDE):
            piece = lax.rem(place_ref[1] - shift - STRIDE * t + 2 * cols, cols)
            odd = lax.rem(piece, 2)
            begin = pl.multiple_of(lax.div(piece, 2) * (TALL + SHORT) + odd * TALL, 8)
            panel_ref[pl.ds(begin, SHORT), :] = ref[t * TALL:t * TALL + SHORT, :]

            @pl.when(odd == 0)
            def _(ref=ref, t=t, begin=begin):
                panel_ref[pl.ds(begin + SHORT, TALL - SHORT), :] = ref[t * TALL + SHORT:(t + 1) * TALL, :]

    high, low = split(panel_ref[...])
    last = (((1,), (1,)), ((), ()))
    out = lax.dot_general(high_ref[...], high, last, preferred_element_type=jnp.float32)
    out += lax.dot_general(low_ref[...], high, last, preferred_element_type=jnp.float32)
    out += lax.dot_general(high_ref[...], low, last, preferred_element_type=jnp.float32)
    out_ref[...] = out.astype(jnp.bfloat16)


def change(place, bundles, solved, here):
    width, n = solved[0].shape
    vmem = pl.BlockSpec(memory_space=pltpu.VMEM)
    return pl.pallas_call(
        change_kernel,
        out_shape=jax.ShapeDtypeStruct((width, here), jnp.bfloat16),
        in_specs=[pl.BlockSpec(memory_space=pltpu.SMEM)] + [vmem] * (len(bundles) + 2),
        out_specs=vmem,
        scratch_shapes=[pltpu.VMEM((here, n), jnp.float32)],
        compiler_params=pltpu.CompilerParams(vmem_limit_bytes=VMEM_LIMIT),
    )(place, *bundles, *solved)


def moved(value, axis, shift):
    size = lax.axis_size(axis)
    return lax.ppermute(value, axis, [(i, (i + shift) % size) for i in range(size)])


def swapped(value, axis, groups=None):
    return lax.all_to_all(value, axis, 0, 0, axis_index_groups=groups, tiled=True)


def copies(value, count):
    return jnp.broadcast_to(value, (count, *value.shape))


def shards(inverse_cov, key_table, weight, edit_index, targets):
    rows = lax.axis_size("row")
    cols = lax.axis_size("col")
    chips = rows // 2
    here = inverse_cov.shape[0]
    n = edit_index.size
    place = jnp.stack([lax.axis_index("row") % 2, lax.axis_index("col")]).astype(jnp.int32)
    turned = [((2 * a + h) * cols + b, (2 * b + h) * cols + a) for a in range(chips) for b in range(cols) for h in range(2)]
    same_core = [[2 * k + h for k in range(chips)] for h in range(2)]
    other_core = [(r, r ^ 1) for r in range(rows)]

    other, mine, key_slice = front(place, edit_index, key_table.T, inverse_cov, weight.T, chips)
    half_sum = mine + lax.ppermute(other, "row", other_core)
    key_piece = lax.ppermute(key_slice, ("row", "col"), turned)
    panel_piece, value_piece, packed = gram_share(swapped(half_sum, "row", same_core), key_piece)

    own = lax.ppermute(panel_piece, ("row", "col"), turned)
    share = packed.shape[0] // rows
    part = jnp.sum(swapped(packed.reshape(rows, share, LANES), "row"), axis=0)
    neighbours = [[STRIDE * g + i for i in range(STRIDE)] for g in range(cols // STRIDE)]
    joined = jnp.concatenate([own, part.reshape(-1, n)], axis=0)
    joined, value_piece = lax.optimization_barrier((joined, value_piece))
    values = swapped(copies(value_piece, rows), "row")
    joined = [joined] + [moved(joined, "col", STRIDE * t) for t in range(1, cols // STRIDE)]
    values, *joined = lax.optimization_barrier((values, *joined))
    far = [item[:TALL] for item in joined]
    part = sum(item[TALL:] for item in joined).reshape(share, LANES)
    part = jnp.sum(swapped(copies(part, STRIDE), "col", neighbours), axis=0)
    gram = swapped(copies(part, rows), "row")
    far = jnp.concatenate(far, axis=0)
    bundles = [far] + [moved(far, "col", shift) for shift in SHIFTS[1:]]
    solved = solve(gram.reshape(rows * share, LANES), jnp.swapaxes(targets, 1, 2), values)
    return change(place, bundles, solved, here).T


def solution(mesh):
    in_specs = (P("row", "col"), P(None, "row"), P("row", "col"), P(), P(None, None, "col"))
    out_specs = P("row", "col")
    return jax.shard_map(shards, mesh=mesh, in_specs=in_specs, out_specs=out_specs, check_vma=False)
```

```python
import math

import jax
import jax.numpy as jnp
from jax import lax
from jax.experimental import pallas as pl
from jax.experimental.pallas import tpu as pltpu
from jax.sharding import PartitionSpec as P

F = 18432
LANES = 128
HIGHEST = lax.Precision.HIGHEST
VMEM_LIMIT = 48 * 2**20
TALL, SHORT, PADDED = 40, 32, 48
V_SHORT = 24
STRIDE = 4
SHIFTS = (0, 1, 2, -1)


def split(value):
    high = value.astype(jnp.bfloat16)
    return high, (value - high.astype(jnp.float32)).astype(jnp.bfloat16)


def dot16(a, b):
    return jnp.dot(a, b, preferred_element_type=jnp.float32)


def solve_kernel(mine_ref, other_ref, target_hbm, high_out, low_out, gram_ref, a_ref, a16_ref, z_ref, s_ref, r_ref, y_ref, target_ref, sem):
    n = a_ref.shape[0]
    width = r_ref.shape[0]
    target_copy = pltpu.make_async_copy(target_hbm, target_ref, sem)
    target_copy.start()
    core = lax.axis_index("row") % 2
    chips = mine_ref.shape[0]
    share = gram_ref.shape[0] // (2 * chips)
    sources = ((core, mine_ref), (1 - core, other_ref))
    for h, ref in sources:
        for k in range(chips):
            gram_ref[pl.ds(pl.multiple_of((2 * k + h) * share, 8), share), :] = ref[k, :share, :]
    blocks = n // LANES
    rows = lax.broadcasted_iota(jnp.int32, (LANES, LANES), 0)
    cols = lax.broadcasted_iota(jnp.int32, (LANES, LANES), 1)
    eye = jnp.where(rows == cols, 1.0, 0.0).astype(jnp.float32)
    place = 0
    for i in range(blocks):
        for j in range(i + 1):
            block = gram_ref[place * LANES:(place + 1) * LANES, :]
            place += 1
            if i == j:
                a_ref[i * LANES:(i + 1) * LANES, j * LANES:(j + 1) * LANES] = block + eye
            else:
                a_ref[i * LANES:(i + 1) * LANES, j * LANES:(j + 1) * LANES] = block
                a_ref[j * LANES:(j + 1) * LANES, i * LANES:(i + 1) * LANES] = block.T
    a = a_ref[...]
    top = jnp.maximum(jnp.max(jnp.sum(jnp.abs(a), axis=0)), 1.0)
    high = a.astype(jnp.bfloat16)
    a16_ref[0] = high
    a16_ref[1] = (a - high.astype(jnp.float32)).astype(jnp.bfloat16)
    middle = top + 1.0
    span = top - 1.0
    scale = 2.0 * middle * middle - span * span
    first, second = 8.0 * middle / scale, 8.0 / scale
    rho = span * span / scale

    def add_eye(ref, times):
        for i in range(blocks):
            at = slice(i * LANES, (i + 1) * LANES)
            ref[at, at] += eye * times

    def load_residual():
        target_copy.wait()
        per_batch = target_ref.shape[2]
        for b in range(target_ref.shape[0]):
            r_ref[:, b * per_batch:(b + 1) * per_batch] = target_ref[b].astype(jnp.float32)
        tile = (mine_ref.shape[1] - share) * LANES // n
        for h, ref in sources:
            for k in range(chips):
                begin = k // 2 * (2 * tile + V_SHORT) + k % 2 * 2 * tile
                for q in range(n // LANES):
                    row = begin + q // 2 * tile
                    tall = tile if q < 2 or k % 2 == 0 else V_SHORT - tile
                    lanes = pl.ds(pl.multiple_of(h * (n // 2) + q % 2 * LANES, LANES), LANES)
                    at = share + q * tile
                    r_ref[row:row + tall, lanes] -= ref[k, at:at + tall, :]

    def more(carry):
        step, before, worst, limit = carry
        return jnp.logical_and(step < 12, worst * worst > limit * before)

    def finish():
        result = y_ref[...] * math.sqrt(F)
        high, low = split(result)
        high_out[...] = high
        low_out[...] = low

    @pl.when(top <= 32.0)
    def _():
        z_ref[...] = -second * a_ref[...]
        add_eye(z_ref, first)
        s_ref[...] = second * dot16(a16_ref[0], a16_ref[0]) - first * a_ref[...]
        add_eye(s_ref, 1.0)

        def body(rho):
            s16 = s_ref[...].astype(jnp.bfloat16)
            both = dot16(jnp.concatenate([z_ref[...].astype(jnp.bfloat16), s16], axis=0), s16)
            z_ref[...] += both[:n]
            s_ref[...] = both[n:]
            return rho * rho

        lax.while_loop(lambda rho: rho * rho > 0.004, body, rho)
        z = z_ref[...]
        z16 = (z + dot16(z.astype(jnp.bfloat16), s_ref[...].astype(jnp.bfloat16))).astype(jnp.bfloat16)
        s_ref[...] = z16.astype(jnp.float32)
        load_residual()
        r = r_ref[...]
        start = dot16(r.astype(jnp.bfloat16), z16).astype(jnp.bfloat16)
        residual = r - (dot16(start, a16_ref[0]) + dot16(start, a16_ref[1]))
        y_ref[...] = start.astype(jnp.float32) + dot16(residual.astype(jnp.bfloat16), z16)
        limit = jnp.max(jnp.abs(r)) * 2e-6

        def refine(carry):
            step, _, before, limit = carry
            y = y_ref[...]
            y_high, y_low = split(y)
            residual = r_ref[...] - (
                dot16(y_high, a16_ref[0]) + (dot16(y_low, a16_ref[0]) + dot16(y_high, a16_ref[1]))
            )
            y_ref[...] = y + dot16(residual.astype(jnp.bfloat16), s_ref[...].astype(jnp.bfloat16))
            return step + 1, before, jnp.max(jnp.abs(residual)), limit

        worst = jnp.max(jnp.abs(residual))
        lax.while_loop(more, refine, (jnp.int32(0), worst, jnp.maximum(worst, 1e-30), limit))
        finish()

    @pl.when(top > 32.0)
    def _():
        def full(x, y):
            return jnp.dot(x, y, precision=HIGHEST, preferred_element_type=jnp.float32)

        z_ref[...] = -second * a_ref[...]
        add_eye(z_ref, first)

        def body(carry):
            rho, extra = carry
            s_ref[...] = -full(a_ref[...], z_ref[...])
            add_eye(s_ref, 1.0)
            z_ref[...] += full(z_ref[...], s_ref[...])
            return rho * rho, jnp.where(rho < 0.01, extra + 1, extra)

        lax.while_loop(lambda carry: carry[1] < 2, body, (rho, jnp.int32(0)))
        load_residual()
        y_ref[...] = full(r_ref[...], z_ref[...])
        size = jnp.max(jnp.abs(r_ref[...]))

        def refine(carry):
            step, _, before, limit = carry
            residual = r_ref[...] - full(y_ref[...], a_ref[...])
            y_ref[...] += full(residual, z_ref[...])
            return step + 1, before, jnp.max(jnp.abs(residual)), limit

        lax.while_loop(more, refine, (jnp.int32(0), size, jnp.maximum(size, 1e-30), size * 2e-6))
        finish()


def solve(mine, other, targets):
    batches, width, per_batch = targets.shape
    n = batches * per_batch
    blocks = n // LANES
    square = pltpu.VMEM((n, n), jnp.float32)
    wide = pltpu.VMEM((width, n), jnp.float32)
    vmem = pl.BlockSpec(memory_space=pltpu.VMEM)
    out = jax.ShapeDtypeStruct((width, n), jnp.bfloat16)
    return pl.pallas_call(
        solve_kernel,
        out_shape=(out, out),
        in_specs=[vmem, vmem, pl.BlockSpec(memory_space=pl.ANY)],
        out_specs=(vmem, vmem),
        scratch_shapes=[
            pltpu.VMEM((blocks * (blocks + 1) // 2 * LANES, LANES), jnp.float32),
            square,
            pltpu.VMEM((2, n, n), jnp.bfloat16),
            square,
            square,
            wide,
            wide,
            pltpu.VMEM(targets.shape, targets.dtype),
            pltpu.SemaphoreType.DMA,
        ],
        compiler_params=pltpu.CompilerParams(vmem_limit_bytes=VMEM_LIMIT),
        cost_estimate=pl.CostEstimate(flops=40 * n * n * n, bytes_accessed=4 * 2**20, transcendentals=0),
    )(mine, other, targets)


def contract_first(a, b):
    return lax.dot_general(a, b, (((0,), (0,)), ((), ())), preferred_element_type=jnp.float32)


def piece_start(index):
    return index // 2 * (TALL + SHORT) + index % 2 * TALL


def front_kernel(index_ref, table_ref, cov_ref, weight_ref, other_ref, mine_ref, slice_ref, part_ref, value_ref):
    here, n = table_ref.shape[0], slice_ref.shape[1]
    chips = mine_ref.shape[0]
    share = mine_ref.shape[1] - TALL
    core, col = lax.axis_index("row") % 2, lax.axis_index("col")
    batches, per_batch = index_ref.shape
    spot = lax.broadcasted_iota(jnp.int32, (table_ref.shape[1], per_batch), 0)
    picked = jnp.concatenate(
        [jnp.where(spot == index_ref[b:b + 1, :], 1.0, 0.0).astype(jnp.bfloat16) for b in range(batches)], axis=1
    )
    keys = dot16(table_ref[...], picked).astype(jnp.bfloat16)
    padded = slice_ref.shape[0]
    slot = lax.broadcasted_iota(jnp.int32, (padded, here), 0)
    spot = lax.broadcasted_iota(jnp.int32, (padded, here), 1)
    odd = lax.rem(col, 2)
    first = lax.div(col, 2) * (TALL + SHORT) + odd * TALL
    taken = jnp.logical_and(slot + first == spot, slot < TALL - odd * (TALL - SHORT))
    taken = jnp.where(taken, 1.0, 0.0).astype(jnp.bfloat16)
    slice_ref[...] = dot16(taken, keys).astype(jnp.bfloat16)
    value_ref[...] = dot16(weight_ref[...], keys)
    high, low = split(cov_ref[...])
    part_ref[...] = contract_first(high, keys) + contract_first(low, keys)
    for which, ref in ((core, mine_ref), (1 - core, other_ref)):
        lanes = pl.ds(pl.multiple_of(which * (n // 2), LANES), n // 2)
        for j in range(chips):
            begin = pl.multiple_of(which * here + piece_start(j), 8)
            tall = TALL if j % 2 == 0 else SHORT
            ref[j, :tall, :] = part_ref[pl.ds(begin, tall), :]
            if tall < TALL:
                ref[j, tall:TALL, :] = jnp.zeros((TALL - tall, n), jnp.float32)
            at = j // 2 * (2 * share + V_SHORT) + j % 2 * 2 * share
            second = share if j % 2 == 0 else V_SHORT - share
            ref[j, TALL:, :n // 2] = value_ref[at:at + share, lanes]
            ref[j, TALL:TALL + second, n // 2:] = value_ref[at + share:at + share + second, lanes]
            if second < share:
                ref[j, TALL + second:, n // 2:] = jnp.zeros((share - second, n // 2), jnp.float32)


def front(index, table, cov, weight, chips):
    n = index.size
    width = weight.shape[0]
    share = width // (2 * chips) + 2
    payload = jax.ShapeDtypeStruct((chips, TALL + share, n), jnp.float32)
    vmem = pl.BlockSpec(memory_space=pltpu.VMEM)
    return pl.pallas_call(
        front_kernel,
        out_shape=(payload, payload, jax.ShapeDtypeStruct((PADDED, n), jnp.bfloat16)),
        in_specs=[vmem] * 4,
        out_specs=(vmem, vmem, vmem),
        scratch_shapes=[
            pltpu.VMEM((cov.shape[1], n), jnp.float32),
            pltpu.VMEM((width, n), jnp.float32),
        ],
        compiler_params=pltpu.CompilerParams(vmem_limit_bytes=VMEM_LIMIT),
    )(index, table, cov, weight)


def gram_kernel(received_ref, key_ref, panel_ref, value_ref, packed_ref):
    total = received_ref[0]
    for j in range(1, received_ref.shape[0]):
        total = total + received_ref[j]
    panel = total[:TALL]
    panel_ref[...] = panel
    tile = total.shape[0] - TALL
    for q in range(total.shape[1] // LANES):
        value_ref[q * tile:(q + 1) * tile, :] = total[TALL:, q * LANES:(q + 1) * LANES]
    n = panel.shape[1]
    padded = jnp.concatenate([panel, jnp.zeros((PADDED - TALL, n), jnp.float32)], axis=0)
    high = padded.astype(jnp.bfloat16)
    rest = padded - high.astype(jnp.float32)
    middle, low = split(rest)
    keys = key_ref[...]
    gram = contract_first(keys, high) + (contract_first(keys, middle) + contract_first(keys, low))
    place = 0
    for i in range(n // LANES):
        for j in range(i + 1):
            packed_ref[place * LANES:(place + 1) * LANES, :] = gram[
                i * LANES:(i + 1) * LANES, j * LANES:(j + 1) * LANES
            ]
            place += 1


def gram_share(received, key_piece):
    n = received.shape[2]
    blocks = n // LANES
    vmem = pl.BlockSpec(memory_space=pltpu.VMEM)
    return pl.pallas_call(
        gram_kernel,
        out_shape=(
            jax.ShapeDtypeStruct((TALL, n), jnp.float32),
            jax.ShapeDtypeStruct(((received.shape[1] - TALL) * blocks, LANES), jnp.float32),
            jax.ShapeDtypeStruct((blocks * (blocks + 1) // 2 * LANES, LANES), jnp.float32),
        ),
        in_specs=[vmem] * 2,
        out_specs=(vmem, vmem, vmem),
        compiler_params=pltpu.CompilerParams(vmem_limit_bytes=VMEM_LIMIT),
    )(received, key_piece)


def change_kernel(*refs):
    *bundle_refs, high_ref, low_ref, out_ref, panel_ref = refs
    cols = len(bundle_refs) * STRIDE
    for shift, ref in zip(SHIFTS, bundle_refs):
        for t in range(cols // STRIDE):
            piece = lax.rem(lax.axis_index("col") - shift - STRIDE * t + 2 * cols, cols)
            odd = lax.rem(piece, 2)
            begin = pl.multiple_of(lax.div(piece, 2) * (TALL + SHORT) + odd * TALL, 8)
            panel_ref[pl.ds(begin, SHORT), :] = ref[t * TALL:t * TALL + SHORT, :]

            @pl.when(odd == 0)
            def _(ref=ref, t=t, begin=begin):
                panel_ref[pl.ds(begin + SHORT, TALL - SHORT), :] = ref[t * TALL + SHORT:(t + 1) * TALL, :]

    high, low = split(panel_ref[...])
    last = (((1,), (1,)), ((), ()))
    out = lax.dot_general(high_ref[...], high, last, preferred_element_type=jnp.float32)
    out += lax.dot_general(low_ref[...], high, last, preferred_element_type=jnp.float32)
    out += lax.dot_general(high_ref[...], low, last, preferred_element_type=jnp.float32)
    out_ref[...] = out.astype(jnp.bfloat16)


def change(bundles, solved, here):
    width, n = solved[0].shape
    vmem = pl.BlockSpec(memory_space=pltpu.VMEM)
    return pl.pallas_call(
        change_kernel,
        out_shape=jax.ShapeDtypeStruct((width, here), jnp.bfloat16),
        in_specs=[vmem] * (len(bundles) + 2),
        out_specs=vmem,
        scratch_shapes=[pltpu.VMEM((here, n), jnp.float32)],
        compiler_params=pltpu.CompilerParams(vmem_limit_bytes=VMEM_LIMIT),
    )(*bundles, *solved)


def moved(value, axis, shift):
    size = lax.axis_size(axis)
    return lax.ppermute(value, axis, [(i, (i + shift) % size) for i in range(size)])


def swapped(value, axis, groups=None):
    return lax.all_to_all(value, axis, 0, 0, axis_index_groups=groups, tiled=True)


def copies(value, count):
    return jnp.broadcast_to(value, (count, *value.shape))


def shards(inverse_cov, key_table, weight, edit_index, targets):
    rows = lax.axis_size("row")
    cols = lax.axis_size("col")
    chips = rows // 2
    here = inverse_cov.shape[0]
    n = edit_index.size
    turned = [((2 * a + h) * cols + b, (2 * b + h) * cols + a) for a in range(chips) for b in range(cols) for h in range(2)]
    same_core = [[2 * k + h for k in range(chips)] for h in range(2)]
    other_core = [(r, r ^ 1) for r in range(rows)]

    other, mine, key_slice = front(edit_index, key_table.T, inverse_cov, weight.T, chips)
    half_sum = mine + lax.ppermute(other, "row", other_core)
    key_piece = lax.ppermute(key_slice, ("row", "col"), turned)
    panel_piece, value_piece, packed = gram_share(swapped(half_sum, "row", same_core), key_piece)

    own = lax.ppermute(panel_piece, ("row", "col"), turned)
    share = packed.shape[0] // rows
    part = jnp.sum(swapped(packed.reshape(rows, share, LANES), "row"), axis=0)
    neighbours = [[STRIDE * g + i for i in range(STRIDE)] for g in range(cols // STRIDE)]
    joined = jnp.concatenate([own, part], axis=1)
    joined = [joined] + [moved(joined, "col", STRIDE * t) for t in range(1, cols // STRIDE)]
    joined = lax.optimization_barrier(tuple(joined))
    far = [item[:, :n] for item in joined]
    part = sum(item[:, n:] for item in joined)
    part = jnp.sum(swapped(copies(part, STRIDE), "col", neighbours), axis=0)
    piece = jnp.concatenate([part, value_piece], axis=0)
    mine = swapped(copies(piece, chips), "row", same_core)
    far = jnp.concatenate(far, axis=0)
    bundles = [far] + [moved(far, "col", shift) for shift in SHIFTS[1:]]
    mine, bundles[1], bundles[2] = lax.optimization_barrier((mine, bundles[1], bundles[2]))
    other = lax.ppermute(mine, "row", other_core)
    solved = solve(mine, other, jnp.swapaxes(targets, 1, 2))
    return change(bundles, solved, here).T


def solution(mesh):
    in_specs = (P("row", "col"), P(None, "row"), P("row", "col"), P(), P(None, None, "col"))
    out_specs = P("row", "col")
    return jax.shard_map(shards, mesh=mesh, in_specs=in_specs, out_specs=out_specs, check_vma=False)
```

```python
import math

import jax
import jax.numpy as jnp
from jax import lax
from jax.experimental import pallas as pl
from jax.experimental.pallas import tpu as pltpu
from jax.sharding import PartitionSpec as P

F = 18432
LANES = 128
HIGHEST = lax.Precision.HIGHEST
VMEM_LIMIT = 48 * 2**20
TALL, SHORT, PADDED = 40, 32, 48
V_SHORT = 24
STRIDE = 4
SHIFTS = (0, 1, 2, -1)


def split(value):
    high = value.astype(jnp.bfloat16)
    return high, (value - high.astype(jnp.float32)).astype(jnp.bfloat16)


def dot16(a, b):
    return jnp.dot(a, b, preferred_element_type=jnp.float32)


def solve_kernel(pieces_ref, target_hbm, high_out, low_out, gram_ref, a_ref, a16_ref, z_ref, s_ref, r_ref, y_ref, target_ref, sem):
    n = a_ref.shape[0]
    width = r_ref.shape[0]
    target_copy = pltpu.make_async_copy(target_hbm, target_ref, sem)
    target_copy.start()
    share = gram_ref.shape[0] // pieces_ref.shape[0]
    for r in range(pieces_ref.shape[0]):
        gram_ref[r * share:(r + 1) * share, :] = pieces_ref[r, :share, :]
    blocks = n // LANES
    rows = lax.broadcasted_iota(jnp.int32, (LANES, LANES), 0)
    cols = lax.broadcasted_iota(jnp.int32, (LANES, LANES), 1)
    eye = jnp.where(rows == cols, 1.0, 0.0).astype(jnp.float32)
    place = 0
    for i in range(blocks):
        for j in range(i + 1):
            block = gram_ref[place * LANES:(place + 1) * LANES, :]
            place += 1
            if i == j:
                a_ref[i * LANES:(i + 1) * LANES, j * LANES:(j + 1) * LANES] = block + eye
            else:
                a_ref[i * LANES:(i + 1) * LANES, j * LANES:(j + 1) * LANES] = block
                a_ref[j * LANES:(j + 1) * LANES, i * LANES:(i + 1) * LANES] = block.T
    a = a_ref[...]
    top = jnp.maximum(jnp.max(jnp.sum(jnp.abs(a), axis=0)), 1.0)
    high = a.astype(jnp.bfloat16)
    a16_ref[0] = high
    a16_ref[1] = (a - high.astype(jnp.float32)).astype(jnp.bfloat16)
    middle = top + 1.0
    span = top - 1.0
    scale = 2.0 * middle * middle - span * span
    first, second = 8.0 * middle / scale, 8.0 / scale
    rho = span * span / scale

    def add_eye(ref, times):
        for i in range(blocks):
            at = slice(i * LANES, (i + 1) * LANES)
            ref[at, at] += eye * times

    def load_residual():
        target_copy.wait()
        per_batch = target_ref.shape[2]
        for b in range(target_ref.shape[0]):
            r_ref[:, b * per_batch:(b + 1) * per_batch] = target_ref[b].astype(jnp.float32)
        tile = (pieces_ref.shape[1] - share) * LANES // n
        for r in range(pieces_ref.shape[0]):
            k, h = r // 2, r % 2
            begin = k // 2 * (2 * tile + V_SHORT) + k % 2 * 2 * tile
            for q in range(n // LANES):
                row = begin + q // 2 * tile
                tall = tile if q < 2 or k % 2 == 0 else V_SHORT - tile
                lane = h * (n // 2) + q % 2 * LANES
                at = share + q * tile
                r_ref[row:row + tall, lane:lane + LANES] -= pieces_ref[r, at:at + tall, :]

    def more(carry):
        step, before, worst, limit = carry
        return jnp.logical_and(step < 12, worst * worst > limit * before)

    def finish():
        result = y_ref[...] * math.sqrt(F)
        high, low = split(result)
        high_out[...] = high
        low_out[...] = low

    @pl.when(top <= 32.0)
    def _():
        z_ref[...] = -second * a_ref[...]
        add_eye(z_ref, first)
        s_ref[...] = second * dot16(a16_ref[0], a16_ref[0]) - first * a_ref[...]
        add_eye(s_ref, 1.0)

        def body(rho):
            s16 = s_ref[...].astype(jnp.bfloat16)
            both = dot16(jnp.concatenate([z_ref[...].astype(jnp.bfloat16), s16], axis=0), s16)
            z_ref[...] += both[:n]
            s_ref[...] = both[n:]
            return rho * rho

        lax.while_loop(lambda rho: rho * rho > 0.004, body, rho)
        z = z_ref[...]
        z16 = (z + dot16(z.astype(jnp.bfloat16), s_ref[...].astype(jnp.bfloat16))).astype(jnp.bfloat16)
        s_ref[...] = z16.astype(jnp.float32)
        load_residual()
        r = r_ref[...]
        start = dot16(r.astype(jnp.bfloat16), z16).astype(jnp.bfloat16)
        residual = r - (dot16(start, a16_ref[0]) + dot16(start, a16_ref[1]))
        y_ref[...] = start.astype(jnp.float32) + dot16(residual.astype(jnp.bfloat16), z16)
        limit = jnp.max(jnp.abs(r)) * 2e-6

        def refine(carry):
            step, _, before, limit = carry
            y = y_ref[...]
            y_high, y_low = split(y)
            residual = r_ref[...] - (
                dot16(y_high, a16_ref[0]) + (dot16(y_low, a16_ref[0]) + dot16(y_high, a16_ref[1]))
            )
            y_ref[...] = y + dot16(residual.astype(jnp.bfloat16), s_ref[...].astype(jnp.bfloat16))
            return step + 1, before, jnp.max(jnp.abs(residual)), limit

        worst = jnp.max(jnp.abs(residual))
        lax.while_loop(more, refine, (jnp.int32(0), worst, jnp.maximum(worst, 1e-30), limit))
        finish()

    @pl.when(top > 32.0)
    def _():
        def full(x, y):
            return jnp.dot(x, y, precision=HIGHEST, preferred_element_type=jnp.float32)

        z_ref[...] = -second * a_ref[...]
        add_eye(z_ref, first)

        def body(carry):
            rho, extra = carry
            s_ref[...] = -full(a_ref[...], z_ref[...])
            add_eye(s_ref, 1.0)
            z_ref[...] += full(z_ref[...], s_ref[...])
            return rho * rho, jnp.where(rho < 0.01, extra + 1, extra)

        lax.while_loop(lambda carry: carry[1] < 2, body, (rho, jnp.int32(0)))
        load_residual()
        y_ref[...] = full(r_ref[...], z_ref[...])
        size = jnp.max(jnp.abs(r_ref[...]))

        def refine(carry):
            step, _, before, limit = carry
            residual = r_ref[...] - full(y_ref[...], a_ref[...])
            y_ref[...] += full(residual, z_ref[...])
            return step + 1, before, jnp.max(jnp.abs(residual)), limit

        lax.while_loop(more, refine, (jnp.int32(0), size, jnp.maximum(size, 1e-30), size * 2e-6))
        finish()


def solve(pieces, targets):
    batches, width, per_batch = targets.shape
    n = batches * per_batch
    blocks = n // LANES
    square = pltpu.VMEM((n, n), jnp.float32)
    wide = pltpu.VMEM((width, n), jnp.float32)
    vmem = pl.BlockSpec(memory_space=pltpu.VMEM)
    out = jax.ShapeDtypeStruct((width, n), jnp.bfloat16)
    return pl.pallas_call(
        solve_kernel,
        out_shape=(out, out),
        in_specs=[vmem, pl.BlockSpec(memory_space=pl.ANY)],
        out_specs=(vmem, vmem),
        scratch_shapes=[
            pltpu.VMEM((blocks * (blocks + 1) // 2 * LANES, LANES), jnp.float32),
            square,
            pltpu.VMEM((2, n, n), jnp.bfloat16),
            square,
            square,
            wide,
            wide,
            pltpu.VMEM(targets.shape, targets.dtype),
            pltpu.SemaphoreType.DMA,
        ],
        compiler_params=pltpu.CompilerParams(vmem_limit_bytes=VMEM_LIMIT),
        cost_estimate=pl.CostEstimate(flops=40 * n * n * n, bytes_accessed=4 * 2**20, transcendentals=0),
    )(pieces, targets)


def contract_first(a, b):
    return lax.dot_general(a, b, (((0,), (0,)), ((), ())), preferred_element_type=jnp.float32)


def piece_start(index):
    return index // 2 * (TALL + SHORT) + index % 2 * TALL


def front_kernel(index_ref, table_ref, cov_ref, weight_ref, other_ref, mine_ref, slice_ref, part_ref, value_ref):
    here, n = table_ref.shape[0], slice_ref.shape[1]
    chips = mine_ref.shape[0]
    share = mine_ref.shape[1] - TALL
    core, col = lax.axis_index("row") % 2, lax.axis_index("col")
    batches, per_batch = index_ref.shape
    spot = lax.broadcasted_iota(jnp.int32, (table_ref.shape[1], per_batch), 0)
    picked = jnp.concatenate(
        [jnp.where(spot == index_ref[b:b + 1, :], 1.0, 0.0).astype(jnp.bfloat16) for b in range(batches)], axis=1
    )
    keys = dot16(table_ref[...], picked).astype(jnp.bfloat16)
    padded = slice_ref.shape[0]
    slot = lax.broadcasted_iota(jnp.int32, (padded, here), 0)
    spot = lax.broadcasted_iota(jnp.int32, (padded, here), 1)
    odd = lax.rem(col, 2)
    first = lax.div(col, 2) * (TALL + SHORT) + odd * TALL
    taken = jnp.logical_and(slot + first == spot, slot < TALL - odd * (TALL - SHORT))
    taken = jnp.where(taken, 1.0, 0.0).astype(jnp.bfloat16)
    slice_ref[...] = dot16(taken, keys).astype(jnp.bfloat16)
    value_ref[...] = dot16(weight_ref[...], keys)
    high, low = split(cov_ref[...])
    part_ref[...] = contract_first(high, keys) + contract_first(low, keys)
    for which, ref in ((core, mine_ref), (1 - core, other_ref)):
        lanes = pl.ds(pl.multiple_of(which * (n // 2), LANES), n // 2)
        for j in range(chips):
            begin = pl.multiple_of(which * here + piece_start(j), 8)
            tall = TALL if j % 2 == 0 else SHORT
            ref[j, :tall, :] = part_ref[pl.ds(begin, tall), :]
            if tall < TALL:
                ref[j, tall:TALL, :] = jnp.zeros((TALL - tall, n), jnp.float32)
            at = j // 2 * (2 * share + V_SHORT) + j % 2 * 2 * share
            second = share if j % 2 == 0 else V_SHORT - share
            ref[j, TALL:, :n // 2] = value_ref[at:at + share, lanes]
            ref[j, TALL:TALL + second, n // 2:] = value_ref[at + share:at + share + second, lanes]
            if second < share:
                ref[j, TALL + second:, n // 2:] = jnp.zeros((share - second, n // 2), jnp.float32)


def front(index, table, cov, weight, chips):
    n = index.size
    width = weight.shape[0]
    share = width // (2 * chips) + 2
    payload = jax.ShapeDtypeStruct((chips, TALL + share, n), jnp.float32)
    vmem = pl.BlockSpec(memory_space=pltpu.VMEM)
    return pl.pallas_call(
        front_kernel,
        out_shape=(payload, payload, jax.ShapeDtypeStruct((PADDED, n), jnp.bfloat16)),
        in_specs=[vmem] * 4,
        out_specs=(vmem, vmem, vmem),
        scratch_shapes=[
            pltpu.VMEM((cov.shape[1], n), jnp.float32),
            pltpu.VMEM((width, n), jnp.float32),
        ],
        compiler_params=pltpu.CompilerParams(vmem_limit_bytes=VMEM_LIMIT),
    )(index, table, cov, weight)


def gram_kernel(received_ref, key_ref, panel_ref, value_ref, packed_ref):
    total = received_ref[0]
    for j in range(1, received_ref.shape[0]):
        total = total + received_ref[j]
    panel = total[:TALL]
    panel_ref[...] = panel
    tile = total.shape[0] - TALL
    for q in range(total.shape[1] // LANES):
        value_ref[q * tile:(q + 1) * tile, :] = total[TALL:, q * LANES:(q + 1) * LANES]
    n = panel.shape[1]
    padded = jnp.concatenate([panel, jnp.zeros((PADDED - TALL, n), jnp.float32)], axis=0)
    high = padded.astype(jnp.bfloat16)
    rest = padded - high.astype(jnp.float32)
    middle, low = split(rest)
    keys = key_ref[...]
    gram = contract_first(keys, high) + (contract_first(keys, middle) + contract_first(keys, low))
    place = 0
    for i in range(n // LANES):
        for j in range(i + 1):
            packed_ref[place * LANES:(place + 1) * LANES, :] = gram[
                i * LANES:(i + 1) * LANES, j * LANES:(j + 1) * LANES
            ]
            place += 1


def gram_share(received, key_piece):
    n = received.shape[2]
    blocks = n // LANES
    vmem = pl.BlockSpec(memory_space=pltpu.VMEM)
    return pl.pallas_call(
        gram_kernel,
        out_shape=(
            jax.ShapeDtypeStruct((TALL, n), jnp.float32),
            jax.ShapeDtypeStruct(((received.shape[1] - TALL) * blocks, LANES), jnp.float32),
            jax.ShapeDtypeStruct((blocks * (blocks + 1) // 2 * LANES, LANES), jnp.float32),
        ),
        in_specs=[vmem] * 2,
        out_specs=(vmem, vmem, vmem),
        compiler_params=pltpu.CompilerParams(vmem_limit_bytes=VMEM_LIMIT),
    )(received, key_piece)


def change_kernel(*refs):
    *bundle_refs, high_ref, low_ref, out_ref, panel_ref = refs
    cols = len(bundle_refs) * STRIDE
    for shift, ref in zip(SHIFTS, bundle_refs):
        for t in range(cols // STRIDE):
            piece = lax.rem(lax.axis_index("col") - shift - STRIDE * t + 2 * cols, cols)
            odd = lax.rem(piece, 2)
            begin = pl.multiple_of(lax.div(piece, 2) * (TALL + SHORT) + odd * TALL, 8)
            panel_ref[pl.ds(begin, SHORT), :] = ref[t * TALL:t * TALL + SHORT, :]

            @pl.when(odd == 0)
            def _(ref=ref, t=t, begin=begin):
                panel_ref[pl.ds(begin + SHORT, TALL - SHORT), :] = ref[t * TALL + SHORT:(t + 1) * TALL, :]

    high, low = split(panel_ref[...])
    last = (((1,), (1,)), ((), ()))
    out = lax.dot_general(high_ref[...], high, last, preferred_element_type=jnp.float32)
    out += lax.dot_general(low_ref[...], high, last, preferred_element_type=jnp.float32)
    out += lax.dot_general(high_ref[...], low, last, preferred_element_type=jnp.float32)
    out_ref[...] = out.astype(jnp.bfloat16)


def change(bundles, solved, here):
    width, n = solved[0].shape
    vmem = pl.BlockSpec(memory_space=pltpu.VMEM)
    return pl.pallas_call(
        change_kernel,
        out_shape=jax.ShapeDtypeStruct((width, here), jnp.bfloat16),
        in_specs=[vmem] * (len(bundles) + 2),
        out_specs=vmem,
        scratch_shapes=[pltpu.VMEM((here, n), jnp.float32)],
        compiler_params=pltpu.CompilerParams(vmem_limit_bytes=VMEM_LIMIT),
    )(*bundles, *solved)


def moved(value, axis, shift):
    size = lax.axis_size(axis)
    return lax.ppermute(value, axis, [(i, (i + shift) % size) for i in range(size)])


def swapped(value, axis, groups=None):
    return lax.all_to_all(value, axis, 0, 0, axis_index_groups=groups, tiled=True)


def copies(value, count):
    return jnp.broadcast_to(value, (count, *value.shape))


def shards(inverse_cov, key_table, weight, edit_index, targets):
    rows = lax.axis_size("row")
    cols = lax.axis_size("col")
    chips = rows // 2
    here = inverse_cov.shape[0]
    n = edit_index.size
    turned = [((2 * a + h) * cols + b, (2 * b + h) * cols + a) for a in range(chips) for b in range(cols) for h in range(2)]
    same_core = [[2 * k + h for k in range(chips)] for h in range(2)]
    other_core = [(r, r ^ 1) for r in range(rows)]

    other, mine, key_slice = front(edit_index, key_table.T, inverse_cov, weight.T, chips)
    half_sum = mine + lax.ppermute(other, "row", other_core)
    key_piece = lax.ppermute(key_slice, ("row", "col"), turned)
    panel_piece, value_piece, packed = gram_share(swapped(half_sum, "row", same_core), key_piece)

    own = lax.ppermute(panel_piece, ("row", "col"), turned)
    share = packed.shape[0] // rows
    part = jnp.sum(swapped(packed.reshape(rows, share, LANES), "row"), axis=0)
    neighbours = [[STRIDE * g + i for i in range(STRIDE)] for g in range(cols // STRIDE)]
    joined = jnp.concatenate([own, part], axis=1)
    joined = [joined] + [moved(joined, "col", STRIDE * t) for t in range(1, cols // STRIDE)]
    joined = lax.optimization_barrier(tuple(joined))
    far = [item[:, :n] for item in joined]
    part = sum(item[:, n:] for item in joined)
    part = jnp.sum(swapped(copies(part, STRIDE), "col", neighbours), axis=0)
    piece = jnp.concatenate([part, value_piece], axis=0)
    pieces = swapped(copies(piece, rows), "row")
    far = jnp.concatenate(far, axis=0)
    bundles = [far] + [moved(far, "col", shift) for shift in SHIFTS[1:]]
    solved = solve(pieces, jnp.swapaxes(targets, 1, 2))
    return change(bundles, solved, here).T


def solution(mesh):
    in_specs = (P("row", "col"), P(None, "row"), P("row", "col"), P(), P(None, None, "col"))
    out_specs = P("row", "col")
    return jax.shard_map(shards, mesh=mesh, in_specs=in_specs, out_specs=out_specs, check_vma=False)
```

```python
import math

import jax
import jax.numpy as jnp
from jax import lax
from jax.experimental import pallas as pl
from jax.experimental.pallas import tpu as pltpu
from jax.sharding import PartitionSpec as P

F = 18432
LANES = 128
HIGHEST = lax.Precision.HIGHEST
VMEM_LIMIT = 48 * 2**20
PADDED = 48
PAIRS = 8
STRIDE = 4
SHIFTS = (0, 1, 2, -1)


def split(value):
    high = value.astype(jnp.bfloat16)
    return high, (value - high.astype(jnp.float32)).astype(jnp.bfloat16)


def dot16(a, b):
    return jnp.dot(a, b, preferred_element_type=jnp.float32)


def solve_kernel(pieces_ref, target_hbm, high_out, low_out, gram_ref, a_ref, a16_ref, z_ref, s_ref, r_ref, y_ref, target_ref, sem):
    n = a_ref.shape[0]
    width = r_ref.shape[0]
    target_copy = pltpu.make_async_copy(target_hbm, target_ref, sem)
    target_copy.start()
    share = gram_ref.shape[0] // pieces_ref.shape[0]
    for r in range(pieces_ref.shape[0]):
        gram_ref[r * share:(r + 1) * share, :] = pieces_ref[r, :share, :]
    blocks = n // LANES
    rows = lax.broadcasted_iota(jnp.int32, (LANES, LANES), 0)
    cols = lax.broadcasted_iota(jnp.int32, (LANES, LANES), 1)
    eye = jnp.where(rows == cols, 1.0, 0.0).astype(jnp.float32)
    place = 0
    for i in range(blocks):
        for j in range(i + 1):
            block = gram_ref[place * LANES:(place + 1) * LANES, :]
            place += 1
            if i == j:
                a_ref[i * LANES:(i + 1) * LANES, j * LANES:(j + 1) * LANES] = block + eye
            else:
                a_ref[i * LANES:(i + 1) * LANES, j * LANES:(j + 1) * LANES] = block
                a_ref[j * LANES:(j + 1) * LANES, i * LANES:(i + 1) * LANES] = block.T
    a = a_ref[...]
    top = jnp.maximum(jnp.max(jnp.sum(jnp.abs(a), axis=0)), 1.0)
    high = a.astype(jnp.bfloat16)
    a16_ref[0] = high
    a16_ref[1] = (a - high.astype(jnp.float32)).astype(jnp.bfloat16)
    middle = top + 1.0
    span = top - 1.0
    scale = 2.0 * middle * middle - span * span
    first, second = 8.0 * middle / scale, 8.0 / scale
    rho = span * span / scale

    def add_eye(ref, times):
        for i in range(blocks):
            at = slice(i * LANES, (i + 1) * LANES)
            ref[at, at] += eye * times

    def load_residual():
        target_copy.wait()
        per_batch = target_ref.shape[2]
        for b in range(target_ref.shape[0]):
            r_ref[:, b * per_batch:(b + 1) * per_batch] = target_ref[b].astype(jnp.float32)
        half = n // 2 // LANES
        tall = (pieces_ref.shape[1] - share) // half
        for r in range(pieces_ref.shape[0]):
            k, h = r // 2, r % 2
            for q in range(half):
                lane = (h * half + q) * LANES
                at = share + q * tall
                r_ref[k * tall:(k + 1) * tall, lane:lane + LANES] -= pieces_ref[r, at:at + tall, :]

    def more(carry):
        step, before, worst, limit = carry
        return jnp.logical_and(step < 12, worst * worst > limit * before)

    def finish():
        result = y_ref[...] * math.sqrt(F)
        high, low = split(result)
        high_out[...] = high
        low_out[...] = low

    @pl.when(top <= 32.0)
    def _():
        z_ref[...] = -second * a_ref[...]
        add_eye(z_ref, first)
        s_ref[...] = second * dot16(a16_ref[0], a16_ref[0]) - first * a_ref[...]
        add_eye(s_ref, 1.0)

        def body(rho):
            s16 = s_ref[...].astype(jnp.bfloat16)
            both = dot16(jnp.concatenate([z_ref[...].astype(jnp.bfloat16), s16], axis=0), s16)
            z_ref[...] += both[:n]
            s_ref[...] = both[n:]
            return rho * rho

        lax.while_loop(lambda rho: rho * rho > 0.004, body, rho)
        z = z_ref[...]
        z16 = (z + dot16(z.astype(jnp.bfloat16), s_ref[...].astype(jnp.bfloat16))).astype(jnp.bfloat16)
        s_ref[...] = z16.astype(jnp.float32)
        load_residual()
        r = r_ref[...]
        start = dot16(r.astype(jnp.bfloat16), z16).astype(jnp.bfloat16)
        residual = r - (dot16(start, a16_ref[0]) + dot16(start, a16_ref[1]))
        y_ref[...] = start.astype(jnp.float32) + dot16(residual.astype(jnp.bfloat16), z16)
        limit = jnp.max(jnp.abs(r)) * 2e-6

        def refine(carry):
            step, _, before, limit = carry
            y = y_ref[...]
            y_high, y_low = split(y)
            residual = r_ref[...] - (
                dot16(y_high, a16_ref[0]) + (dot16(y_low, a16_ref[0]) + dot16(y_high, a16_ref[1]))
            )
            y_ref[...] = y + dot16(residual.astype(jnp.bfloat16), s_ref[...].astype(jnp.bfloat16))
            return step + 1, before, jnp.max(jnp.abs(residual)), limit

        worst = jnp.max(jnp.abs(residual))
        lax.while_loop(more, refine, (jnp.int32(0), worst, jnp.maximum(worst, 1e-30), limit))
        finish()

    @pl.when(top > 32.0)
    def _():
        def full(x, y):
            return jnp.dot(x, y, precision=HIGHEST, preferred_element_type=jnp.float32)

        z_ref[...] = -second * a_ref[...]
        add_eye(z_ref, first)

        def body(carry):
            rho, extra = carry
            s_ref[...] = -full(a_ref[...], z_ref[...])
            add_eye(s_ref, 1.0)
            z_ref[...] += full(z_ref[...], s_ref[...])
            return rho * rho, jnp.where(rho < 0.01, extra + 1, extra)

        lax.while_loop(lambda carry: carry[1] < 2, body, (rho, jnp.int32(0)))
        load_residual()
        y_ref[...] = full(r_ref[...], z_ref[...])
        size = jnp.max(jnp.abs(r_ref[...]))

        def refine(carry):
            step, _, before, limit = carry
            residual = r_ref[...] - full(y_ref[...], a_ref[...])
            y_ref[...] += full(residual, z_ref[...])
            return step + 1, before, jnp.max(jnp.abs(residual)), limit

        lax.while_loop(more, refine, (jnp.int32(0), size, jnp.maximum(size, 1e-30), size * 2e-6))
        finish()


def solve(pieces, targets):
    batches, width, per_batch = targets.shape
    n = batches * per_batch
    blocks = n // LANES
    square = pltpu.VMEM((n, n), jnp.float32)
    wide = pltpu.VMEM((width, n), jnp.float32)
    vmem = pl.BlockSpec(memory_space=pltpu.VMEM)
    out = jax.ShapeDtypeStruct((width, n), jnp.bfloat16)
    return pl.pallas_call(
        solve_kernel,
        out_shape=(out, out),
        in_specs=[vmem, pl.BlockSpec(memory_space=pl.ANY)],
        out_specs=(vmem, vmem),
        scratch_shapes=[
            pltpu.VMEM((blocks * (blocks + 1) // 2 * LANES, LANES), jnp.float32),
            square,
            pltpu.VMEM((2, n, n), jnp.bfloat16),
            square,
            square,
            wide,
            wide,
            pltpu.VMEM(targets.shape, targets.dtype),
            pltpu.SemaphoreType.DMA,
        ],
        compiler_params=pltpu.CompilerParams(vmem_limit_bytes=VMEM_LIMIT),
        cost_estimate=pl.CostEstimate(flops=40 * n * n * n, bytes_accessed=4 * 2**20, transcendentals=0),
    )(pieces, targets)


def contract_first(a, b):
    return lax.dot_general(a, b, (((0,), (0,)), ((), ())), preferred_element_type=jnp.float32)


def front_kernel(index_ref, table_ref, cov_hbm, weight_ref, other_ref, mine_ref, slice_ref, cov_ref, part_ref, value_ref, sem):
    load = pltpu.make_async_copy(cov_hbm, cov_ref, sem)
    load.start()
    here, n = table_ref.shape[0], slice_ref.shape[1]
    chips = mine_ref.shape[0]
    core, col = lax.axis_index("row") % 2, lax.axis_index("col")
    batches, per_batch = index_ref.shape
    spot = lax.broadcasted_iota(jnp.int32, (table_ref.shape[1], per_batch), 0)
    picked = jnp.concatenate(
        [jnp.where(spot == index_ref[b:b + 1, :], 1.0, 0.0).astype(jnp.bfloat16) for b in range(batches)], axis=1
    )
    keys = dot16(table_ref[...], picked).astype(jnp.bfloat16)
    padded = slice_ref.shape[0]
    slot = lax.broadcasted_iota(jnp.int32, (padded, here), 0)
    spot = lax.broadcasted_iota(jnp.int32, (padded, here), 1)
    tall = here // chips
    taken = jnp.logical_and(slot + col * tall == spot, slot < tall)
    taken = jnp.where(taken, 1.0, 0.0).astype(jnp.bfloat16)
    slice_ref[...] = dot16(taken, keys).astype(jnp.bfloat16)
    value = dot16(weight_ref[...], keys)
    load.wait()
    high, low = split(cov_ref[...])
    part = contract_first(high, keys) + contract_first(low, keys)
    for h in range(2):
        value_ref[h] = value[:, h * (n // 2):(h + 1) * (n // 2)]
        part_ref[h] = part[h * here:(h + 1) * here]
    wide = weight_ref.shape[0] // chips
    for which, ref in ((core, mine_ref), (1 - core, other_ref)):
        for j in range(chips):
            at = 0
            for q in range(n // LANES):
                ref[j, at:at + tall, :] = part_ref[which, j * tall:(j + 1) * tall, q * LANES:(q + 1) * LANES]
                at += tall
            for q in range(n // 2 // LANES):
                ref[j, at:at + wide, :] = value_ref[which, j * wide:(j + 1) * wide, q * LANES:(q + 1) * LANES]
                at += wide


def front(index, table, cov, weight, chips):
    n = index.size
    here, width = table.shape[0], weight.shape[0]
    blocks = n // LANES
    rows = here // chips * blocks + width // chips * blocks // 2
    payload = jax.ShapeDtypeStruct((chips, rows, LANES), jnp.float32)
    vmem = pl.BlockSpec(memory_space=pltpu.VMEM)
    return pl.pallas_call(
        front_kernel,
        out_shape=(payload, payload, jax.ShapeDtypeStruct((PADDED, n), jnp.bfloat16)),
        in_specs=[vmem, vmem, pl.BlockSpec(memory_space=pltpu.HBM), vmem],
        out_specs=(vmem, vmem, vmem),
        scratch_shapes=[
            pltpu.VMEM(cov.shape, cov.dtype),
            pltpu.VMEM((2, here, n), jnp.float32),
            pltpu.VMEM((2, width, n // 2), jnp.float32),
            pltpu.SemaphoreType.DMA,
        ],
        compiler_params=pltpu.CompilerParams(vmem_limit_bytes=VMEM_LIMIT),
    )(index, table, cov, weight)


def gram_kernel(received_ref, key_ref, panel_ref, value_ref, packed_ref):
    total = received_ref[0]
    for j in range(1, received_ref.shape[0]):
        total = total + received_ref[j]
    rows = panel_ref.shape[0]
    panel_ref[...] = total[:rows]
    value_ref[...] = total[rows:]
    keys = key_ref[...]
    n = keys.shape[1]
    tall = rows * LANES // n
    panel = jnp.concatenate([total[q * tall:(q + 1) * tall] for q in range(n // LANES)], axis=1)
    padded = jnp.concatenate([panel, jnp.zeros((PADDED - tall, n), jnp.float32)], axis=0)
    high = padded.astype(jnp.bfloat16)
    rest = padded - high.astype(jnp.float32)
    middle, low = split(rest)
    gram = contract_first(keys, high) + (contract_first(keys, middle) + contract_first(keys, low))
    place = 0
    for i in range(n // LANES):
        for j in range(i + 1):
            packed_ref[place * LANES:(place + 1) * LANES, :] = gram[
                i * LANES:(i + 1) * LANES, j * LANES:(j + 1) * LANES
            ]
            place += 1


def gram_share(received, key_piece, rows):
    blocks = key_piece.shape[1] // LANES
    vmem = pl.BlockSpec(memory_space=pltpu.VMEM)
    return pl.pallas_call(
        gram_kernel,
        out_shape=(
            jax.ShapeDtypeStruct((rows, LANES), jnp.float32),
            jax.ShapeDtypeStruct((received.shape[1] - rows, LANES), jnp.float32),
            jax.ShapeDtypeStruct((blocks * (blocks + 1) // 2 * LANES, LANES), jnp.float32),
        ),
        in_specs=[vmem] * 2,
        out_specs=(vmem, vmem, vmem),
        compiler_params=pltpu.CompilerParams(vmem_limit_bytes=VMEM_LIMIT),
    )(received, key_piece)


def change_kernel(*refs):
    *bundle_refs, high_ref, low_ref, out_ref, panel_ref = refs
    cols = len(bundle_refs) * STRIDE
    blocks, tall = high_ref.shape[1] // LANES, out_ref.shape[1] // cols
    for shift, ref in zip(SHIFTS, bundle_refs):
        for t in range(cols // STRIDE):
            piece = lax.rem(lax.axis_index("col") - shift - STRIDE * t + 2 * cols, cols)
            for parity in range(2):

                @pl.when(lax.rem(piece, 2) == parity)
                def _(ref=ref, t=t, pair=lax.div(piece, 2), parity=parity):
                    for q in range(blocks):
                        at = (t * blocks + q) * tall
                        panel_ref[pair, parity * tall:(parity + 1) * tall, q * LANES:(q + 1) * LANES] = ref[at:at + tall, :]

    high, low = split(panel_ref[...].reshape(out_ref.shape[1], blocks * LANES))
    last = (((1,), (1,)), ((), ()))
    out = lax.dot_general(high_ref[...], high, last, preferred_element_type=jnp.float32)
    out += lax.dot_general(low_ref[...], high, last, preferred_element_type=jnp.float32)
    out += lax.dot_general(high_ref[...], low, last, preferred_element_type=jnp.float32)
    out_ref[...] = out.astype(jnp.bfloat16)


def change(bundles, solved, here):
    width, n = solved[0].shape
    vmem = pl.BlockSpec(memory_space=pltpu.VMEM)
    return pl.pallas_call(
        change_kernel,
        out_shape=jax.ShapeDtypeStruct((width, here), jnp.bfloat16),
        in_specs=[vmem] * (len(bundles) + 2),
        out_specs=vmem,
        scratch_shapes=[pltpu.VMEM((PAIRS, here // PAIRS, n), jnp.float32)],
        compiler_params=pltpu.CompilerParams(vmem_limit_bytes=VMEM_LIMIT),
    )(*bundles, *solved)


def moved(value, axis, shift):
    size = lax.axis_size(axis)
    return lax.ppermute(value, axis, [(i, (i + shift) % size) for i in range(size)])


def swapped(value, axis, groups=None):
    return lax.all_to_all(value, axis, 0, 0, axis_index_groups=groups, tiled=True)


def copies(value, count):
    return jnp.broadcast_to(value, (count, *value.shape))


def shards(inverse_cov, key_table, weight, edit_index, targets):
    rows = lax.axis_size("row")
    cols = lax.axis_size("col")
    chips = rows // 2
    here = inverse_cov.shape[0]
    n = edit_index.size
    turned = [((2 * a + h) * cols + b, (2 * b + h) * cols + a) for a in range(chips) for b in range(cols) for h in range(2)]
    same_core = [[2 * k + h for k in range(chips)] for h in range(2)]
    other_core = [(r, r ^ 1) for r in range(rows)]

    other, mine, key_slice = front(edit_index, key_table.T, inverse_cov, weight.T, chips)
    half_sum = mine + lax.ppermute(other, "row", other_core)
    key_piece = lax.ppermute(key_slice, ("row", "col"), turned)
    panel_piece, value_piece, packed = gram_share(
        swapped(half_sum, "row", same_core), key_piece, here // chips * (n // LANES)
    )

    own = lax.ppermute(panel_piece, ("row", "col"), turned)
    share = packed.shape[0] // rows
    part = jnp.sum(swapped(packed.reshape(rows, share, LANES), "row"), axis=0)
    neighbours = [[STRIDE * g + i for i in range(STRIDE)] for g in range(cols // STRIDE)]
    joined = jnp.concatenate([own, part], axis=0)
    joined = [joined] + [moved(joined, "col", STRIDE * t) for t in range(1, cols // STRIDE)]
    joined = lax.optimization_barrier(tuple(joined))
    far = [item[:-share] for item in joined]
    part = sum(item[-share:] for item in joined)
    part = jnp.sum(swapped(copies(part, STRIDE), "col", neighbours), axis=0)
    piece = jnp.concatenate([part, value_piece], axis=0)
    pieces = swapped(copies(piece, rows), "row")
    far = jnp.concatenate(far, axis=0)
    bundles = [far] + [moved(far, "col", shift) for shift in SHIFTS[1:]]
    solved = solve(pieces, jnp.swapaxes(targets, 1, 2))
    return change(bundles, solved, here).T


def solution(mesh):
    in_specs = (P("row", "col"), P(None, "row"), P("row", "col"), P(), P(None, None, "col"))
    out_specs = P("row", "col")
    return jax.shard_map(shards, mesh=mesh, in_specs=in_specs, out_specs=out_specs, check_vma=False)
```

```python
import math

import jax
import jax.numpy as jnp
from jax import lax
from jax.experimental import pallas as pl
from jax.experimental.pallas import tpu as pltpu
from jax.sharding import PartitionSpec as P

F = 18432
LANES = 128
HIGHEST = lax.Precision.HIGHEST
VMEM_LIMIT = 48 * 2**20
PADDED = 48
PAIRS = 8
STRIDE = 4
SHIFTS = (0, 1, 2, -1)


def split(value):
    high = value.astype(jnp.bfloat16)
    return high, (value - high.astype(jnp.float32)).astype(jnp.bfloat16)


def dot16(a, b):
    return jnp.dot(a, b, preferred_element_type=jnp.float32)


def solve_kernel(pieces_ref, target_hbm, high_out, low_out, gram_ref, a_ref, a16_ref, z_ref, s_ref, r_ref, y_ref, target_ref, sem):
    n = a_ref.shape[0]
    width = r_ref.shape[0]
    target_copy = pltpu.make_async_copy(target_hbm, target_ref, sem)
    target_copy.start()
    share = gram_ref.shape[0] // pieces_ref.shape[0]
    for r in range(pieces_ref.shape[0]):
        gram_ref[r * share:(r + 1) * share, :] = pieces_ref[r, :share, :]
    blocks = n // LANES
    rows = lax.broadcasted_iota(jnp.int32, (LANES, LANES), 0)
    cols = lax.broadcasted_iota(jnp.int32, (LANES, LANES), 1)
    eye = jnp.where(rows == cols, 1.0, 0.0).astype(jnp.float32)
    place = 0
    for i in range(blocks):
        for j in range(i + 1):
            block = gram_ref[place * LANES:(place + 1) * LANES, :]
            place += 1
            if i == j:
                a_ref[i * LANES:(i + 1) * LANES, j * LANES:(j + 1) * LANES] = block + eye
            else:
                a_ref[i * LANES:(i + 1) * LANES, j * LANES:(j + 1) * LANES] = block
                a_ref[j * LANES:(j + 1) * LANES, i * LANES:(i + 1) * LANES] = block.T
    a = a_ref[...]
    top = jnp.maximum(jnp.max(jnp.sum(jnp.abs(a), axis=0)), 1.0)
    high = a.astype(jnp.bfloat16)
    a16_ref[0] = high
    a16_ref[1] = (a - high.astype(jnp.float32)).astype(jnp.bfloat16)
    middle = top + 1.0
    span = top - 1.0
    scale = 2.0 * middle * middle - span * span
    first, second = 8.0 * middle / scale, 8.0 / scale
    rho = span * span / scale

    def add_eye(ref, times):
        for i in range(blocks):
            at = slice(i * LANES, (i + 1) * LANES)
            ref[at, at] += eye * times

    def load_residual():
        target_copy.wait()
        per_batch = target_ref.shape[2]
        for b in range(target_ref.shape[0]):
            r_ref[:, b * per_batch:(b + 1) * per_batch] = target_ref[b].astype(jnp.float32)
        half = n // 2 // LANES
        tall = (pieces_ref.shape[1] - share) // half
        for r in range(pieces_ref.shape[0]):
            k, h = r // 2, r % 2
            for q in range(half):
                lane = (h * half + q) * LANES
                at = share + q * tall
                r_ref[k * tall:(k + 1) * tall, lane:lane + LANES] -= pieces_ref[r, at:at + tall, :]

    def more(carry):
        step, before, worst, limit = carry
        return jnp.logical_and(step < 12, worst * worst > limit * before)

    def finish():
        result = y_ref[...] * math.sqrt(F)
        high, low = split(result)
        high_out[...] = high
        low_out[...] = low

    @pl.when(top <= 32.0)
    def _():
        z_ref[...] = -second * a_ref[...]
        add_eye(z_ref, first)
        s_ref[...] = second * dot16(a16_ref[0], a16_ref[0]) - first * a_ref[...]
        add_eye(s_ref, 1.0)

        def body(rho):
            s16 = s_ref[...].astype(jnp.bfloat16)
            both = dot16(jnp.concatenate([z_ref[...].astype(jnp.bfloat16), s16], axis=0), s16)
            z_ref[...] += both[:n]
            s_ref[...] = both[n:]
            return rho * rho

        lax.while_loop(lambda rho: rho * rho > 0.004, body, rho)
        z = z_ref[...]
        z16 = (z + dot16(z.astype(jnp.bfloat16), s_ref[...].astype(jnp.bfloat16))).astype(jnp.bfloat16)
        s_ref[...] = z16.astype(jnp.float32)
        load_residual()
        r = r_ref[...]
        start = dot16(r.astype(jnp.bfloat16), z16).astype(jnp.bfloat16)
        residual = r - (dot16(start, a16_ref[0]) + dot16(start, a16_ref[1]))
        y_ref[...] = start.astype(jnp.float32) + dot16(residual.astype(jnp.bfloat16), z16)
        limit = jnp.max(jnp.abs(r)) * 2e-6

        def refine(carry):
            step, _, before, limit = carry
            y = y_ref[...]
            y_high, y_low = split(y)
            residual = r_ref[...] - (
                dot16(y_high, a16_ref[0]) + (dot16(y_low, a16_ref[0]) + dot16(y_high, a16_ref[1]))
            )
            y_ref[...] = y + dot16(residual.astype(jnp.bfloat16), s_ref[...].astype(jnp.bfloat16))
            return step + 1, before, jnp.max(jnp.abs(residual)), limit

        worst = jnp.max(jnp.abs(residual))
        lax.while_loop(more, refine, (jnp.int32(0), worst, jnp.maximum(worst, 1e-30), limit))
        finish()

    @pl.when(top > 32.0)
    def _():
        def full(x, y):
            return jnp.dot(x, y, precision=HIGHEST, preferred_element_type=jnp.float32)

        z_ref[...] = -second * a_ref[...]
        add_eye(z_ref, first)

        def body(carry):
            rho, extra = carry
            s_ref[...] = -full(a_ref[...], z_ref[...])
            add_eye(s_ref, 1.0)
            z_ref[...] += full(z_ref[...], s_ref[...])
            return rho * rho, jnp.where(rho < 0.01, extra + 1, extra)

        lax.while_loop(lambda carry: carry[1] < 2, body, (rho, jnp.int32(0)))
        load_residual()
        y_ref[...] = full(r_ref[...], z_ref[...])
        size = jnp.max(jnp.abs(r_ref[...]))

        def refine(carry):
            step, _, before, limit = carry
            residual = r_ref[...] - full(y_ref[...], a_ref[...])
            y_ref[...] += full(residual, z_ref[...])
            return step + 1, before, jnp.max(jnp.abs(residual)), limit

        lax.while_loop(more, refine, (jnp.int32(0), size, jnp.maximum(size, 1e-30), size * 2e-6))
        finish()


def solve(pieces, targets):
    batches, width, per_batch = targets.shape
    n = batches * per_batch
    blocks = n // LANES
    square = pltpu.VMEM((n, n), jnp.float32)
    wide = pltpu.VMEM((width, n), jnp.float32)
    vmem = pl.BlockSpec(memory_space=pltpu.VMEM)
    out = jax.ShapeDtypeStruct((width, n), jnp.bfloat16)
    return pl.pallas_call(
        solve_kernel,
        out_shape=(out, out),
        in_specs=[vmem, pl.BlockSpec(memory_space=pl.ANY)],
        out_specs=(vmem, vmem),
        scratch_shapes=[
            pltpu.VMEM((blocks * (blocks + 1) // 2 * LANES, LANES), jnp.float32),
            square,
            pltpu.VMEM((2, n, n), jnp.bfloat16),
            square,
            square,
            wide,
            wide,
            pltpu.VMEM(targets.shape, targets.dtype),
            pltpu.SemaphoreType.DMA,
        ],
        compiler_params=pltpu.CompilerParams(vmem_limit_bytes=VMEM_LIMIT),
        cost_estimate=pl.CostEstimate(flops=40 * n * n * n, bytes_accessed=4 * 2**20, transcendentals=0),
    )(pieces, targets)


def contract_first(a, b):
    return lax.dot_general(a, b, (((0,), (0,)), ((), ())), preferred_element_type=jnp.float32)


def front_kernel(index_ref, table_ref, cov_hbm, weight_ref, other_ref, mine_ref, slice_ref, cov_ref, part_ref, value_ref, sem):
    load = pltpu.make_async_copy(cov_hbm, cov_ref, sem)
    load.start()
    here, n = table_ref.shape[0], slice_ref.shape[1]
    chips = mine_ref.shape[0]
    core, col = lax.axis_index("row") % 2, lax.axis_index("col")
    batches, per_batch = index_ref.shape
    spot = lax.broadcasted_iota(jnp.int32, (table_ref.shape[1], per_batch), 0)
    picked = jnp.concatenate(
        [jnp.where(spot == index_ref[b:b + 1, :], 1.0, 0.0).astype(jnp.bfloat16) for b in range(batches)], axis=1
    )
    keys = dot16(table_ref[...], picked).astype(jnp.bfloat16)
    padded = slice_ref.shape[0]
    slot = lax.broadcasted_iota(jnp.int32, (padded, here), 0)
    spot = lax.broadcasted_iota(jnp.int32, (padded, here), 1)
    tall = here // chips
    taken = jnp.logical_and(slot + col * tall == spot, slot < tall)
    taken = jnp.where(taken, 1.0, 0.0).astype(jnp.bfloat16)
    slice_ref[...] = dot16(taken, keys).astype(jnp.bfloat16)
    value = dot16(weight_ref[...], keys)
    load.wait()
    high, low = split(cov_ref[...])
    part = contract_first(high, keys) + contract_first(low, keys)
    for h in range(2):
        value_ref[h] = value[:, h * (n // 2):(h + 1) * (n // 2)]
        part_ref[h] = part[h * here:(h + 1) * here]
    wide = weight_ref.shape[0] // chips
    for which, ref in ((core, mine_ref), (1 - core, other_ref)):
        for j in range(chips):
            at = 0
            for q in range(n // LANES):
                ref[j, at:at + tall, :] = part_ref[which, j * tall:(j + 1) * tall, q * LANES:(q + 1) * LANES]
                at += tall
            for q in range(n // 2 // LANES):
                ref[j, at:at + wide, :] = value_ref[which, j * wide:(j + 1) * wide, q * LANES:(q + 1) * LANES]
                at += wide


def front(index, table, cov, weight, chips):
    n = index.size
    here, width = table.shape[0], weight.shape[0]
    blocks = n // LANES
    rows = here // chips * blocks + width // chips * blocks // 2
    payload = jax.ShapeDtypeStruct((chips, rows, LANES), jnp.float32)
    vmem = pl.BlockSpec(memory_space=pltpu.VMEM)
    return pl.pallas_call(
        front_kernel,
        out_shape=(payload, payload, jax.ShapeDtypeStruct((PADDED, n), jnp.bfloat16)),
        in_specs=[vmem, vmem, pl.BlockSpec(memory_space=pltpu.HBM), vmem],
        out_specs=(vmem, vmem, vmem),
        scratch_shapes=[
            pltpu.VMEM(cov.shape, cov.dtype),
            pltpu.VMEM((2, here, n), jnp.float32),
            pltpu.VMEM((2, width, n // 2), jnp.float32),
            pltpu.SemaphoreType.DMA,
        ],
        compiler_params=pltpu.CompilerParams(vmem_limit_bytes=VMEM_LIMIT),
    )(index, table, cov, weight)


def gram_kernel(received_ref, key_ref, panel_ref, value_ref, packed_ref):
    total = received_ref[0]
    for j in range(1, received_ref.shape[0]):
        total = total + received_ref[j]
    rows = panel_ref.shape[0]
    panel_ref[...] = total[:rows]
    value_ref[...] = total[rows:]
    keys = key_ref[...]
    n = keys.shape[1]
    tall = rows * LANES // n
    panel = jnp.concatenate([total[q * tall:(q + 1) * tall] for q in range(n // LANES)], axis=1)
    padded = jnp.concatenate([panel, jnp.zeros((PADDED - tall, n), jnp.float32)], axis=0)
    high = padded.astype(jnp.bfloat16)
    rest = padded - high.astype(jnp.float32)
    middle, low = split(rest)
    gram = contract_first(keys, high) + (contract_first(keys, middle) + contract_first(keys, low))
    place = 0
    for i in range(n // LANES):
        for j in range(i + 1):
            packed_ref[place * LANES:(place + 1) * LANES, :] = gram[
                i * LANES:(i + 1) * LANES, j * LANES:(j + 1) * LANES
            ]
            place += 1


def gram_share(received, key_piece, rows):
    blocks = key_piece.shape[1] // LANES
    vmem = pl.BlockSpec(memory_space=pltpu.VMEM)
    return pl.pallas_call(
        gram_kernel,
        out_shape=(
            jax.ShapeDtypeStruct((rows, LANES), jnp.float32),
            jax.ShapeDtypeStruct((received.shape[1] - rows, LANES), jnp.float32),
            jax.ShapeDtypeStruct((blocks * (blocks + 1) // 2 * LANES, LANES), jnp.float32),
        ),
        in_specs=[vmem] * 2,
        out_specs=(vmem, vmem, vmem),
        compiler_params=pltpu.CompilerParams(vmem_limit_bytes=VMEM_LIMIT),
    )(received, key_piece)


def change_kernel(*refs):
    *bundle_refs, high_ref, low_ref, out_ref, panel_ref = refs
    cols = len(bundle_refs) * STRIDE
    blocks, tall = high_ref.shape[1] // LANES, out_ref.shape[1] // cols
    for shift, ref in zip(SHIFTS, bundle_refs):
        for t in range(cols // STRIDE):
            piece = lax.rem(lax.axis_index("col") - shift - STRIDE * t + 2 * cols, cols)
            for parity in range(2):

                @pl.when(lax.rem(piece, 2) == parity)
                def _(ref=ref, t=t, pair=lax.div(piece, 2), parity=parity):
                    for q in range(blocks):
                        at = (t * blocks + q) * tall
                        panel_ref[pair, parity * tall:(parity + 1) * tall, q * LANES:(q + 1) * LANES] = ref[at:at + tall, :]

    high, low = split(panel_ref[...].reshape(out_ref.shape[1], blocks * LANES))
    last = (((1,), (1,)), ((), ()))
    out = lax.dot_general(high_ref[...], high, last, preferred_element_type=jnp.float32)
    out += lax.dot_general(low_ref[...], high, last, preferred_element_type=jnp.float32)
    out += lax.dot_general(high_ref[...], low, last, preferred_element_type=jnp.float32)
    out_ref[...] = out.astype(jnp.bfloat16)


def change(bundles, solved, here):
    width, n = solved[0].shape
    vmem = pl.BlockSpec(memory_space=pltpu.VMEM)
    return pl.pallas_call(
        change_kernel,
        out_shape=jax.ShapeDtypeStruct((width, here), jnp.bfloat16),
        in_specs=[vmem] * (len(bundles) + 2),
        out_specs=vmem,
        scratch_shapes=[pltpu.VMEM((PAIRS, here // PAIRS, n), jnp.float32)],
        compiler_params=pltpu.CompilerParams(vmem_limit_bytes=VMEM_LIMIT),
    )(*bundles, *solved)


def moved(value, axis, shift):
    size = lax.axis_size(axis)
    return lax.ppermute(value, axis, [(i, (i + shift) % size) for i in range(size)])


def swapped(value, axis, groups=None):
    return lax.all_to_all(value, axis, 0, 0, axis_index_groups=groups, tiled=True)


def copies(value, count):
    return jnp.broadcast_to(value, (count, *value.shape))


def shards(inverse_cov, key_table, weight, edit_index, targets):
    rows = lax.axis_size("row")
    cols = lax.axis_size("col")
    chips = rows // 2
    here = inverse_cov.shape[0]
    n = edit_index.size
    turned = [((2 * a + h) * cols + b, (2 * b + h) * cols + a) for a in range(chips) for b in range(cols) for h in range(2)]
    same_core = [[2 * k + h for k in range(chips)] for h in range(2)]
    other_core = [(r, r ^ 1) for r in range(rows)]

    other, mine, key_slice = front(edit_index, key_table.T, inverse_cov, weight.T, chips)
    half_sum = mine + lax.ppermute(other, "row", other_core)
    key_piece = lax.ppermute(key_slice, ("row", "col"), turned)
    panel_piece, value_piece, packed = gram_share(
        swapped(half_sum, "row", same_core), key_piece, here // chips * (n // LANES)
    )

    own = lax.ppermute(panel_piece, ("row", "col"), turned)
    share = packed.shape[0] // rows
    part = jnp.sum(swapped(packed.reshape(rows, share, LANES), "row"), axis=0)
    neighbours = [[STRIDE * g + i for i in range(STRIDE)] for g in range(cols // STRIDE)]
    part, own = lax.optimization_barrier((part, own))
    part = jnp.sum(swapped(copies(part, STRIDE), "col", neighbours), axis=0)
    joined = jnp.concatenate([own, part], axis=0)
    joined = [joined] + [moved(joined, "col", STRIDE * t) for t in range(1, cols // STRIDE)]
    joined = lax.optimization_barrier(tuple(joined))
    far = [item[:-share] for item in joined]
    part = sum(item[-share:] for item in joined)
    piece = jnp.concatenate([part, value_piece], axis=0)
    pieces = swapped(copies(piece, rows), "row")
    far = jnp.concatenate(far, axis=0)
    bundles = [far] + [moved(far, "col", shift) for shift in SHIFTS[1:]]
    solved = solve(pieces, jnp.swapaxes(targets, 1, 2))
    return change(bundles, solved, here).T


def solution(mesh):
    in_specs = (P("row", "col"), P(None, "row"), P("row", "col"), P(), P(None, None, "col"))
    out_specs = P("row", "col")
    return jax.shard_map(shards, mesh=mesh, in_specs=in_specs, out_specs=out_specs, check_vma=False)
```

```python
import math

import jax
import jax.numpy as jnp
from jax import lax
from jax.experimental import pallas as pl
from jax.experimental.pallas import tpu as pltpu
from jax.sharding import PartitionSpec as P

F = 18432
LANES = 128
HIGHEST = lax.Precision.HIGHEST
VMEM_LIMIT = 48 * 2**20
PADDED = 48
PAIRS = 8
STRIDE = 4
SHIFTS = (0, 1, 2, -1)


def split(value):
    high = value.astype(jnp.bfloat16)
    return high, (value - high.astype(jnp.float32)).astype(jnp.bfloat16)


def dot16(a, b):
    return jnp.dot(a, b, preferred_element_type=jnp.float32)


def solve_kernel(pieces_ref, target_hbm, high_out, low_out, gram_ref, a_ref, a16_ref, z_ref, s_ref, r_ref, y_ref, target_ref, sem):
    n = a_ref.shape[0]
    width = r_ref.shape[0]
    target_copy = pltpu.make_async_copy(target_hbm, target_ref, sem)
    target_copy.start()
    share = gram_ref.shape[0] // pieces_ref.shape[0]
    for r in range(pieces_ref.shape[0]):
        gram_ref[r * share:(r + 1) * share, :] = pieces_ref[r, :share, :]
    blocks = n // LANES
    rows = lax.broadcasted_iota(jnp.int32, (LANES, LANES), 0)
    cols = lax.broadcasted_iota(jnp.int32, (LANES, LANES), 1)
    eye = jnp.where(rows == cols, 1.0, 0.0).astype(jnp.float32)
    place = 0
    for i in range(blocks):
        for j in range(i + 1):
            block = gram_ref[place * LANES:(place + 1) * LANES, :]
            place += 1
            if i == j:
                a_ref[i * LANES:(i + 1) * LANES, j * LANES:(j + 1) * LANES] = block + eye
            else:
                a_ref[i * LANES:(i + 1) * LANES, j * LANES:(j + 1) * LANES] = block
                a_ref[j * LANES:(j + 1) * LANES, i * LANES:(i + 1) * LANES] = block.T
    a = a_ref[...]
    top = jnp.maximum(jnp.max(jnp.sum(jnp.abs(a), axis=0)), 1.0)
    high = a.astype(jnp.bfloat16)
    a16_ref[0] = high
    a16_ref[1] = (a - high.astype(jnp.float32)).astype(jnp.bfloat16)
    middle = top + 1.0
    span = top - 1.0
    scale = 2.0 * middle * middle - span * span
    first, second = 8.0 * middle / scale, 8.0 / scale
    rho = span * span / scale

    def add_eye(ref, times):
        for i in range(blocks):
            at = slice(i * LANES, (i + 1) * LANES)
            ref[at, at] += eye * times

    def load_residual():
        target_copy.wait()
        per_batch = target_ref.shape[2]
        for b in range(target_ref.shape[0]):
            r_ref[:, b * per_batch:(b + 1) * per_batch] = target_ref[b].astype(jnp.float32)
        half = n // 2 // LANES
        tall = (pieces_ref.shape[1] - share) // half
        for r in range(pieces_ref.shape[0]):
            k, h = r // 2, r % 2
            for q in range(half):
                lane = (h * half + q) * LANES
                at = share + q * tall
                r_ref[k * tall:(k + 1) * tall, lane:lane + LANES] -= pieces_ref[r, at:at + tall, :]

    def more(carry):
        step, before, worst, limit = carry
        return jnp.logical_and(step < 12, worst * worst > limit * before)

    def finish():
        result = y_ref[...] * math.sqrt(F)
        high, low = split(result)
        high_out[...] = high
        low_out[...] = low

    @pl.when(top <= 32.0)
    def _():
        z_ref[...] = -second * a_ref[...]
        add_eye(z_ref, first)
        s_ref[...] = second * dot16(a16_ref[0], a16_ref[0]) - first * a_ref[...]
        add_eye(s_ref, 1.0)

        def body(rho):
            s16 = s_ref[...].astype(jnp.bfloat16)
            both = dot16(jnp.concatenate([z_ref[...].astype(jnp.bfloat16), s16], axis=0), s16)
            z_ref[...] += both[:n]
            s_ref[...] = both[n:]
            return rho * rho

        lax.while_loop(lambda rho: rho * rho > 0.004, body, rho)
        z = z_ref[...]
        z16 = (z + dot16(z.astype(jnp.bfloat16), s_ref[...].astype(jnp.bfloat16))).astype(jnp.bfloat16)
        s_ref[...] = z16.astype(jnp.float32)
        load_residual()
        r = r_ref[...]
        start = dot16(r.astype(jnp.bfloat16), z16).astype(jnp.bfloat16)
        residual = r - (dot16(start, a16_ref[0]) + dot16(start, a16_ref[1]))
        y_ref[...] = start.astype(jnp.float32) + dot16(residual.astype(jnp.bfloat16), z16)
        limit = jnp.max(jnp.abs(r)) * 2e-6

        def refine(carry):
            step, _, before, limit = carry
            y = y_ref[...]
            y_high, y_low = split(y)
            residual = r_ref[...] - (
                dot16(y_high, a16_ref[0]) + (dot16(y_low, a16_ref[0]) + dot16(y_high, a16_ref[1]))
            )
            y_ref[...] = y + dot16(residual.astype(jnp.bfloat16), s_ref[...].astype(jnp.bfloat16))
            return step + 1, before, jnp.max(jnp.abs(residual)), limit

        worst = jnp.max(jnp.abs(residual))
        lax.while_loop(more, refine, (jnp.int32(0), worst, jnp.maximum(worst, 1e-30), limit))
        finish()

    @pl.when(top > 32.0)
    def _():
        def full(x, y):
            return jnp.dot(x, y, precision=HIGHEST, preferred_element_type=jnp.float32)

        z_ref[...] = -second * a_ref[...]
        add_eye(z_ref, first)

        def body(carry):
            rho, extra = carry
            s_ref[...] = -full(a_ref[...], z_ref[...])
            add_eye(s_ref, 1.0)
            z_ref[...] += full(z_ref[...], s_ref[...])
            return rho * rho, jnp.where(rho < 0.01, extra + 1, extra)

        lax.while_loop(lambda carry: carry[1] < 2, body, (rho, jnp.int32(0)))
        load_residual()
        y_ref[...] = full(r_ref[...], z_ref[...])
        size = jnp.max(jnp.abs(r_ref[...]))

        def refine(carry):
            step, _, before, limit = carry
            residual = r_ref[...] - full(y_ref[...], a_ref[...])
            y_ref[...] += full(residual, z_ref[...])
            return step + 1, before, jnp.max(jnp.abs(residual)), limit

        lax.while_loop(more, refine, (jnp.int32(0), size, jnp.maximum(size, 1e-30), size * 2e-6))
        finish()


def solve(pieces, targets):
    batches, width, per_batch = targets.shape
    n = batches * per_batch
    blocks = n // LANES
    square = pltpu.VMEM((n, n), jnp.float32)
    wide = pltpu.VMEM((width, n), jnp.float32)
    vmem = pl.BlockSpec(memory_space=pltpu.VMEM)
    out = jax.ShapeDtypeStruct((width, n), jnp.bfloat16)
    return pl.pallas_call(
        solve_kernel,
        out_shape=(out, out),
        in_specs=[vmem, pl.BlockSpec(memory_space=pl.ANY)],
        out_specs=(vmem, vmem),
        scratch_shapes=[
            pltpu.VMEM((blocks * (blocks + 1) // 2 * LANES, LANES), jnp.float32),
            square,
            pltpu.VMEM((2, n, n), jnp.bfloat16),
            square,
            square,
            wide,
            wide,
            pltpu.VMEM(targets.shape, targets.dtype),
            pltpu.SemaphoreType.DMA,
        ],
        compiler_params=pltpu.CompilerParams(vmem_limit_bytes=VMEM_LIMIT),
        cost_estimate=pl.CostEstimate(flops=40 * n * n * n, bytes_accessed=4 * 2**20, transcendentals=0),
    )(pieces, targets)


def contract_first(a, b):
    return lax.dot_general(a, b, (((0,), (0,)), ((), ())), preferred_element_type=jnp.float32)


def front_kernel(index_ref, table_ref, cov_hbm, weight_ref, other_ref, mine_ref, slice_ref, cov_ref, part_ref, value_ref, sem):
    load = pltpu.make_async_copy(cov_hbm, cov_ref, sem)
    load.start()
    here, n = table_ref.shape[0], slice_ref.shape[1]
    chips = mine_ref.shape[0]
    core, col = lax.axis_index("row") % 2, lax.axis_index("col")
    batches, per_batch = index_ref.shape
    spot = lax.broadcasted_iota(jnp.int32, (table_ref.shape[1], per_batch), 0)
    picked = jnp.concatenate(
        [jnp.where(spot == index_ref[b:b + 1, :], 1.0, 0.0).astype(jnp.bfloat16) for b in range(batches)], axis=1
    )
    keys = dot16(table_ref[...], picked).astype(jnp.bfloat16)
    padded = slice_ref.shape[0]
    slot = lax.broadcasted_iota(jnp.int32, (padded, here), 0)
    spot = lax.broadcasted_iota(jnp.int32, (padded, here), 1)
    tall = here // chips
    taken = jnp.logical_and(slot + col * tall == spot, slot < tall)
    taken = jnp.where(taken, 1.0, 0.0).astype(jnp.bfloat16)
    slice_ref[...] = dot16(taken, keys).astype(jnp.bfloat16)
    value = dot16(weight_ref[...], keys)
    load.wait()
    high, low = split(cov_ref[...])
    part = contract_first(high, keys) + contract_first(low, keys)
    for h in range(2):
        value_ref[h] = value[:, h * (n // 2):(h + 1) * (n // 2)]
        part_ref[h] = part[h * here:(h + 1) * here]
    wide = weight_ref.shape[0] // chips
    for which, ref in ((core, mine_ref), (1 - core, other_ref)):
        for j in range(chips):
            at = 0
            for q in range(n // LANES):
                ref[j, at:at + tall, :] = part_ref[which, j * tall:(j + 1) * tall, q * LANES:(q + 1) * LANES]
                at += tall
            for q in range(n // 2 // LANES):
                ref[j, at:at + wide, :] = value_ref[which, j * wide:(j + 1) * wide, q * LANES:(q + 1) * LANES]
                at += wide


def front(index, table, cov, weight, chips):
    n = index.size
    here, width = table.shape[0], weight.shape[0]
    blocks = n // LANES
    rows = here // chips * blocks + width // chips * blocks // 2
    payload = jax.ShapeDtypeStruct((chips, rows, LANES), jnp.float32)
    vmem = pl.BlockSpec(memory_space=pltpu.VMEM)
    return pl.pallas_call(
        front_kernel,
        out_shape=(payload, payload, jax.ShapeDtypeStruct((PADDED, n), jnp.bfloat16)),
        in_specs=[vmem, vmem, pl.BlockSpec(memory_space=pltpu.HBM), vmem],
        out_specs=(vmem, vmem, vmem),
        scratch_shapes=[
            pltpu.VMEM(cov.shape, cov.dtype),
            pltpu.VMEM((2, here, n), jnp.float32),
            pltpu.VMEM((2, width, n // 2), jnp.float32),
            pltpu.SemaphoreType.DMA,
        ],
        compiler_params=pltpu.CompilerParams(vmem_limit_bytes=VMEM_LIMIT),
    )(index, table, cov, weight)


def gram_kernel(received_ref, key_ref, panel_ref, value_ref, packed_ref):
    total = received_ref[0]
    for j in range(1, received_ref.shape[0]):
        total = total + received_ref[j]
    rows = panel_ref.shape[0]
    panel_ref[...] = total[:rows]
    value_ref[...] = total[rows:]
    keys = key_ref[...]
    n = keys.shape[1]
    tall = rows * LANES // n
    panel = jnp.concatenate([total[q * tall:(q + 1) * tall] for q in range(n // LANES)], axis=1)
    padded = jnp.concatenate([panel, jnp.zeros((PADDED - tall, n), jnp.float32)], axis=0)
    high = padded.astype(jnp.bfloat16)
    rest = padded - high.astype(jnp.float32)
    middle, low = split(rest)
    gram = contract_first(keys, high) + (contract_first(keys, middle) + contract_first(keys, low))
    place = 0
    for i in range(n // LANES):
        for j in range(i + 1):
            packed_ref[place * LANES:(place + 1) * LANES, :] = gram[
                i * LANES:(i + 1) * LANES, j * LANES:(j + 1) * LANES
            ]
            place += 1


def gram_share(received, key_piece, rows):
    blocks = key_piece.shape[1] // LANES
    vmem = pl.BlockSpec(memory_space=pltpu.VMEM)
    return pl.pallas_call(
        gram_kernel,
        out_shape=(
            jax.ShapeDtypeStruct((rows, LANES), jnp.float32),
            jax.ShapeDtypeStruct((received.shape[1] - rows, LANES), jnp.float32),
            jax.ShapeDtypeStruct((blocks * (blocks + 1) // 2 * LANES, LANES), jnp.float32),
        ),
        in_specs=[vmem] * 2,
        out_specs=(vmem, vmem, vmem),
        compiler_params=pltpu.CompilerParams(vmem_limit_bytes=VMEM_LIMIT),
    )(received, key_piece)


def change_kernel(*refs):
    *bundle_refs, high_ref, low_ref, out_ref, panel_ref = refs
    cols = len(bundle_refs) * STRIDE
    blocks, tall = high_ref.shape[1] // LANES, out_ref.shape[1] // cols
    for shift, ref in zip(SHIFTS, bundle_refs):
        for t in range(cols // STRIDE):
            piece = lax.rem(lax.axis_index("col") - shift - STRIDE * t + 2 * cols, cols)
            for parity in range(2):

                @pl.when(lax.rem(piece, 2) == parity)
                def _(ref=ref, t=t, pair=lax.div(piece, 2), parity=parity):
                    for q in range(blocks):
                        at = (t * blocks + q) * tall
                        panel_ref[pair, parity * tall:(parity + 1) * tall, q * LANES:(q + 1) * LANES] = ref[at:at + tall, :]

    high, low = split(panel_ref[...].reshape(out_ref.shape[1], blocks * LANES))
    last = (((1,), (1,)), ((), ()))
    out = lax.dot_general(high_ref[...], high, last, preferred_element_type=jnp.float32)
    out += lax.dot_general(low_ref[...], high, last, preferred_element_type=jnp.float32)
    out += lax.dot_general(high_ref[...], low, last, preferred_element_type=jnp.float32)
    out_ref[...] = out.astype(jnp.bfloat16)


def change(bundles, solved, here):
    width, n = solved[0].shape
    vmem = pl.BlockSpec(memory_space=pltpu.VMEM)
    return pl.pallas_call(
        change_kernel,
        out_shape=jax.ShapeDtypeStruct((width, here), jnp.bfloat16),
        in_specs=[vmem] * (len(bundles) + 2),
        out_specs=vmem,
        scratch_shapes=[pltpu.VMEM((PAIRS, here // PAIRS, n), jnp.float32)],
        compiler_params=pltpu.CompilerParams(vmem_limit_bytes=VMEM_LIMIT),
    )(*bundles, *solved)


def moved(value, axis, shift):
    size = lax.axis_size(axis)
    return lax.ppermute(value, axis, [(i, (i + shift) % size) for i in range(size)])


def swapped(value, axis, groups=None):
    return lax.all_to_all(value, axis, 0, 0, axis_index_groups=groups, tiled=True)


def copies(value, count):
    return jnp.broadcast_to(value, (count, *value.shape))


def shards(inverse_cov, key_table, weight, edit_index, targets):
    rows = lax.axis_size("row")
    cols = lax.axis_size("col")
    chips = rows // 2
    here = inverse_cov.shape[0]
    n = edit_index.size
    turned = [((2 * a + h) * cols + b, (2 * b + h) * cols + a) for a in range(chips) for b in range(cols) for h in range(2)]
    same_core = [[2 * k + h for k in range(chips)] for h in range(2)]
    other_core = [(r, r ^ 1) for r in range(rows)]

    other, mine, key_slice = front(edit_index, key_table.T, inverse_cov, weight.T, chips)
    half_sum = mine + lax.ppermute(other, "row", other_core)
    key_piece = lax.ppermute(key_slice, ("row", "col"), turned)
    panel_piece, value_piece, packed = gram_share(
        swapped(half_sum, "row", same_core), key_piece, here // chips * (n // LANES)
    )

    own = lax.ppermute(panel_piece, ("row", "col"), turned)
    share = packed.shape[0] // rows
    part = jnp.sum(swapped(packed.reshape(rows, share, LANES), "row"), axis=0)
    part = part + sum(moved(part, "col", shift) for shift in SHIFTS[1:])
    joined = jnp.concatenate([own, part], axis=0)
    joined = [joined] + [moved(joined, "col", STRIDE * t) for t in range(1, cols // STRIDE)]
    joined = lax.optimization_barrier(tuple(joined))
    far = [item[:-share] for item in joined]
    part = sum(item[-share:] for item in joined)
    piece = jnp.concatenate([part, value_piece], axis=0)
    pieces = swapped(copies(piece, rows), "row")
    far = jnp.concatenate(far, axis=0)
    bundles = [far] + [moved(far, "col", shift) for shift in SHIFTS[1:]]
    solved = solve(pieces, jnp.swapaxes(targets, 1, 2))
    return change(bundles, solved, here).T


def solution(mesh):
    in_specs = (P("row", "col"), P(None, "row"), P("row", "col"), P(), P(None, None, "col"))
    out_specs = P("row", "col")
    return jax.shard_map(shards, mesh=mesh, in_specs=in_specs, out_specs=out_specs, check_vma=False)
```
